128 devices in a mesh: replica: 16 (over x_hi, y, core), tensor: 8 (over z, x_lo).
Axes of the slice: x: 4 (x_hi: 2, x_lo: 2; x = x_hi * 2 + x_lo), y: 4, z: 4, core: 2. Of those that a mesh axis runs over, the one named last changes fastest.
Arguments:
- queries: bfloat16 [16, 128, 2, 8192], P('replica', None, None, 'tensor'), may hold values from -110 to 110
- step_key_value: bfloat16 [16, 128, 2, 2, 1024], P('replica', None, None, None, 'tensor'), may hold values from -4.1 to 4.1
- replica_page_store: bfloat16 [16, 2, 128, 64, 1024], P('replica', None, None, None, 'tensor'), may hold values from -4 to 4
- page_table: int32 [16, 128, 16], P('replica'), may hold values from 0 to 127
- lengths: int32 [16, 128], P('replica'), may hold values from 1 to 1024, 81920 in all within a row
- mig_offset: int32 [16, 14, 1], P('replica'), may hold values from 0 to 14; in each aligned block of 14 rows (0 to 13, 14 to 27, ..., all dimensions but the last counted through in order) at most 2 rows name the same one
- copy_order: int32 [16, 14, 16], P('replica'), may hold values from 0 to 15, each once within a row
- out_weight: bfloat16 [8192, 8192], P('tensor'), may hold values from -0.0625 to 0.0625
Outputs:
- attention: bfloat16 [16, 128, 2, 8192], P('replica', None, None, 'tensor')
- projected: bfloat16 [16, 128, 2, 8192], P('replica', 'tensor')
- arrived: bfloat16 [16, 14, 4, 2, 64, 1024], P('replica', None, None, None, None, 'tensor')
The draws below stay inside these ranges and needn't reach their ends.
Inputs may be any that keep to these rules, and one draw needn't show every extreme that they name: Row 114 + j of replica r arrived from replica (r + 1 + mig_offset[r, j, 0]) mod 16; at most 2 of one replica's arriving rows come from one source. `page_table`: entries name pages of the pool of the row's home replica; pages may be shared. `lengths`: each replica has a row of exactly 1024 tokens. `copy_order`: each row is an ordering of its 16 pages.
All inputs are finite; a program needn't handle non-finite values.
Results may differ from the reference program's by a relative error of at most 0.019.
Values may be sent and summed in bfloat16 or wider, within the bound.
No kernel may reach another device: no remote copies, remote signals or barrier semaphores. Data moves between devices by JAX's collectives and lax.ppermute only.
A program may use at most 384 MiB of HBM per device.

```python
import math
import jax
import jax.numpy as jnp
import numpy as np
from jax import lax

D = 8192
QUERY_HEADS = 64
KEY_VALUE_HEADS = 8
HEAD_SIZE = 128
DECODE_ROWS = 128
MIGRANTS = 14
PAGE_TOKENS = 64
PAGES_ROW = 16
REPLICA_PAGES = 128
COPIED = 4
CAP = 2
N_REPLICA = 16


def draw_queries(key, part):
    key = jax.random.fold_in(key, 3)
    first_key = jax.random.fold_in(key, 0)
    value_rows = 2.0 * jnp.clip(jax.random.normal(first_key, (N_REPLICA, DECODE_ROWS, 2, QUERY_HEADS * HEAD_SIZE), jnp.float32), -4.0, 4.0)
    return value_rows.astype(jnp.bfloat16)


def draw_step_key_value(key, part):
    key = jax.random.fold_in(key, 7)
    value_rows = jnp.clip(jax.random.normal(key, (N_REPLICA, DECODE_ROWS, 2, 2, KEY_VALUE_HEADS * HEAD_SIZE), jnp.float32), -4.0, 4.0)
    return value_rows.astype(jnp.bfloat16)


def plant(result, stream_key, least, largest):
    longest = result.shape.index(max(result.shape))
    spots = []
    for shift in (0, 1):
        where = [jax.random.randint(jax.random.fold_in(stream_key, axis), (), 0, length) for axis, length in enumerate(result.shape)]
        where[longest] = (where[longest] + shift) % result.shape[longest]
        spots.append(tuple(where))
    return result.at[spots[0]].set(least).at[spots[1]].set(largest)


def block_scale(stream_key, shape, pieces, low, high):
    factor_of, own = 1.0, jax.random.fold_in(stream_key, 6)
    for dim, parts in pieces:
        draws = jnp.exp(jax.random.uniform(jax.random.fold_in(own, dim), (parts,), jnp.float32, low / len(pieces), high / len(pieces)))
        factor_of = factor_of * jnp.repeat(draws, shape[dim] // parts).reshape([-1 if axis == dim else 1 for axis in range(len(shape))])
    return factor_of


def profile(count, total, reach, skew):
    weights = [(1 << 20) // math.isqrt(rank ** skew) + 1 for rank in range(2, count + 1)]
    rest, given = total - reach - (count - 1), [1] * (count - 1)
    while rest > 0:
        candidates = [i for i in range(count - 1) if given[i] < reach]
        whole, remaining = sum([weights[i] for i in candidates]), rest
        for i in candidates:
            more = min(reach - given[i], max(1, remaining * weights[i] // whole), rest)
            given[i] = given[i] + more
            rest = rest - more
    return np.array([reach] + given)


def uneven_parts(stream_key, count, total, reach, slope):
    if count == 2:
        one = jax.random.randint(stream_key, (), max(1, total - reach), min(reach, total - 1) + 1)
        return jnp.stack([one, total - one])
    tallies = jnp.asarray(profile(count, total, reach, slope), jnp.int32)
    couples = (count - 1) // 2
    donor, sink = tallies[1:1 + 2 * couples:2], tallies[2:2 + 2 * couples:2]
    slack = jnp.minimum(donor - 1, reach - sink)
    passed = jax.random.randint(jax.random.fold_in(stream_key, 1), (couples,), 0, 1 << 20) % (slack + 1)
    tallies = tallies.at[1:1 + 2 * couples:2].set(donor - passed).at[2:2 + 2 * couples:2].set(sink + passed)
    return tallies[jax.random.permutation(jax.random.fold_in(stream_key, 2), count)]


def shared_out(key, own, number, rows, number_of, top, most, slope):
    ranking = jax.random.permutation(key, number_of)
    packed, usual = portions_of(number_of, rows * top, most, slope, True), portions_of(number_of, rows * top, most, slope, False)
    places = jnp.arange(number_of)

    def named(sizes, offset_by):
        used = int((sizes > 0).sum())
        fixed = max(1, used // 4)
        passed = fixed + (places - fixed + offset_by * (used - fixed)) % max(1, number_of - fixed)
        return jnp.zeros((number_of,), jnp.int32).at[ranking[jnp.where(places < fixed, places, passed)]].set(jnp.asarray(sizes, jnp.int32))

    sizes = jnp.where(number % 4 == 0, named(packed, number // 4), named(usual, number - number // 4 - 1))
    mixed = jax.random.permutation(jax.random.fold_in(own, 3), number_of)
    donor, sink = mixed[0:number_of // 2 * 2:2], mixed[1:number_of // 2 * 2:2]
    room = jnp.minimum(sizes[donor] - 1, most - sizes[sink]) // 2
    room = jnp.where((donor == ranking[0]) | (sink == ranking[0]) | (sizes[sink] == 0), 0, jnp.maximum(room, 0))
    passed = jax.random.randint(jax.random.fold_in(own, 4), (number_of // 2,), 0, 1 << 20) % (room + 1)
    sizes = sizes.at[donor].add(-passed).at[sink].add(passed)
    members = jnp.searchsorted(jnp.cumsum(sizes), jnp.arange(rows * top), side="right").astype(jnp.int32)
    table = members.reshape(top, rows).T
    table = table[jax.random.permutation(jax.random.fold_in(own, 1), rows)]
    offset_by = jax.random.randint(jax.random.fold_in(own, 2), (rows, 1), 0, top)
    return jnp.take_along_axis(table, (jnp.arange(top)[None, :] + offset_by) % top, axis=1)


def portions_of(count, total, limit, skew, full):
    portions = [(1 << 20) // math.isqrt(standing ** skew) + 1 for standing in range(1, count + 1)]
    largest = limit if full else min(limit, max(-(-total // count), total * portions[0] // sum(portions)))
    least = 1 if total - largest >= count - 1 else 0
    given, spare = [largest] + [least] * (count - 1), total - largest - least * (count - 1)
    while spare > 0:
        movable = [i for i in range(1, count) if given[i] < largest] or [i for i in range(1, count) if given[i] < limit]
        mass, budget = sum([portions[i] for i in movable]), spare
        for i in movable:
            extra = min(limit - given[i], max(1, budget * portions[i] // mass), spare)
            given[i] = given[i] + extra
            spare = spare - extra
    return np.array(given)


def noise(own_key, shape, spread, bound, cuts=(), kind=jnp.bfloat16):
    level = block_scale(own_key, shape, cuts, -0.22, 0.18) if cuts else 1.0
    values = jax.random.normal(own_key, shape, jnp.float32) * spread * level
    return jnp.minimum(jnp.maximum(values, -bound), bound).astype(kind)


def setup_inputs(seed: int = 0) -> dict:
    key_list = jax.random.split(jax.random.key(seed), 9)
    queries = draw_queries(jax.random.fold_in(key_list[8], 71), 0)
    step_key_value = draw_step_key_value(jax.random.fold_in(key_list[8], 71), 0)
    replica_page_store = noise(key_list[2], (N_REPLICA * 1, 2, REPLICA_PAGES, PAGE_TOKENS, KEY_VALUE_HEADS * HEAD_SIZE), 1.0, 4.0, ((0, 16), (4, 8)))
    page_table = plant(jax.random.randint(key_list[3], (N_REPLICA * 1, DECODE_ROWS, PAGES_ROW), 0, REPLICA_PAGES), jax.random.fold_in(key_list[3], 1), 0, REPLICA_PAGES - 1).astype(jnp.int32)
    lengths = jax.vmap(lambda own: uneven_parts(own, DECODE_ROWS, DECODE_ROWS * PAGES_ROW * PAGE_TOKENS * 5 // 8, PAGES_ROW * PAGE_TOKENS, 1))(jax.random.split(key_list[4], (N_REPLICA * 1))).reshape((N_REPLICA * 1, DECODE_ROWS)).astype(jnp.int32)
    mig_offset_keys = jax.random.split(jax.random.fold_in(key_list[5], 1), (N_REPLICA * 1) * MIGRANTS // MIGRANTS)
    mig_offset_turns = jax.random.permutation(jax.random.fold_in(key_list[5], 3), (N_REPLICA * 1) * MIGRANTS // MIGRANTS)
    mig_offset = jax.vmap(lambda own, number: shared_out(jax.random.fold_in(key_list[5], 2), own, number, MIGRANTS, N_REPLICA - 1, 1, CAP, 2))(mig_offset_keys, mig_offset_turns).reshape((N_REPLICA * 1, MIGRANTS, 1))
    copy_order = jax.vmap(lambda own: jax.random.permutation(own, PAGES_ROW))(jax.random.split(key_list[6], (N_REPLICA * 1) * MIGRANTS)).reshape((N_REPLICA * 1, MIGRANTS, PAGES_ROW)).astype(jnp.int32)
    out_weight = noise(key_list[7], (QUERY_HEADS * HEAD_SIZE, D), (QUERY_HEADS * HEAD_SIZE) ** -0.5, 0.0625, ((0, 8),))
    return dict(queries=queries, step_key_value=step_key_value, replica_page_store=replica_page_store, page_table=page_table, lengths=lengths, mig_offset=mig_offset, copy_order=copy_order, out_weight=out_weight)


NEG_FILL = -1e+30

def replica_rows(inputs, replica_page_store):
    queries, step_key_value, page_table, lengths, home_of = inputs
    query_group_size = QUERY_HEADS // KEY_VALUE_HEADS
    context_length = PAGES_ROW * PAGE_TOKENS
    selected_pages = replica_page_store[home_of[:, None], :, page_table]
    cached_page_keys = selected_pages[:, :, 0].reshape(DECODE_ROWS, context_length, KEY_VALUE_HEADS, HEAD_SIZE)
    cached_page_values = selected_pages[:, :, 1].reshape(DECODE_ROWS, context_length, KEY_VALUE_HEADS, HEAD_SIZE)
    fresh_token = step_key_value.reshape(DECODE_ROWS, 2, 2, KEY_VALUE_HEADS, HEAD_SIZE)
    all_keys = jnp.concatenate([cached_page_keys, fresh_token[:, :, 0]], axis=1).astype(jnp.float32)
    all_values = jnp.concatenate([cached_page_values, fresh_token[:, :, 1]], axis=1).astype(jnp.float32)
    query_head_vectors = queries.reshape(DECODE_ROWS, 2, KEY_VALUE_HEADS, query_group_size, HEAD_SIZE).astype(jnp.float32)
    scores = jnp.einsum('rsgjd,rkgd->rsgjk', query_head_vectors, all_keys, precision=lax.Precision.HIGHEST) / math.sqrt(HEAD_SIZE)
    position = jnp.arange(context_length + 2, dtype=jnp.int32)
    step_index = jnp.arange(2, dtype=jnp.int32)
    allowed = jnp.where(position[None, None, :] < context_length, position[None, None, :] < lengths[:, None, None], position[None, None, :] - context_length <= step_index[None, :, None])
    allowed = allowed[:, :, None, None, :]
    masked = jnp.where(allowed, scores, NEG_FILL)
    highest = lax.optimization_barrier(jnp.max(masked, axis=-1, keepdims=True))
    weights = jnp.where(allowed, jnp.exp(masked - highest), 0.0).astype(jnp.bfloat16)
    weights = lax.optimization_barrier(weights).astype(jnp.float32)
    total = lax.optimization_barrier(jnp.sum(weights, axis=-1))
    weighted = jnp.einsum('rsgjk,rkgd->rsgjd', weights, all_values, precision=lax.Precision.HIGHEST)
    return (weighted / total[..., None]).astype(jnp.bfloat16).reshape(DECODE_ROWS, 2, QUERY_HEADS * HEAD_SIZE)

def reference(queries, step_key_value, replica_page_store, page_table, lengths, mig_offset, copy_order, out_weight):
    replica_ids = jnp.arange(N_REPLICA, dtype=jnp.int32)
    source_of = (replica_ids[:, None] + 1 + mig_offset[:, :, 0]) % N_REPLICA
    home_of = jnp.concatenate([jnp.broadcast_to(replica_ids[:, None], (N_REPLICA, DECODE_ROWS - MIGRANTS)), source_of], axis=1)
    attention = lax.map(lambda inputs: replica_rows(inputs, replica_page_store), (queries, step_key_value, page_table, lengths, home_of))
    projected = jnp.dot(attention.reshape(-1, QUERY_HEADS * HEAD_SIZE), out_weight, preferred_element_type=jnp.float32)
    projected = projected.astype(jnp.bfloat16).reshape(N_REPLICA, DECODE_ROWS, 2, D)
    wanted = jnp.take_along_axis(page_table[:, DECODE_ROWS - MIGRANTS:], copy_order[:, :, :COPIED], axis=2)
    arrived = replica_page_store[source_of[:, :, None], :, wanted]
    return (attention, projected, arrived)
```

```python
import functools
import math

import jax
import jax.numpy as jnp
from jax import lax
from jax.experimental import pallas as pl
from jax.experimental.pallas import tpu as pltpu
from jax.sharding import PartitionSpec as P

HEAD = 128
ROWS = 128
MIGRANTS = 14
STAYING = ROWS - MIGRANTS
COPIED = 4
PAGES_ROW = 16
PAGE = 64
REPLICAS = 16
CAP = 2
SLOTS = REPLICAS * CAP
GROUP = 8
CONTEXT = PAGES_ROW * PAGE
NEG_FILL = -1e30
SCALE = math.log2(math.e) / math.sqrt(HEAD)
META_ROW = 4
PIECES = 2
VMEM = pl.BlockSpec(memory_space=pltpu.VMEM)
SMEM = pl.BlockSpec(memory_space=pltpu.SMEM)
HBM = pl.BlockSpec(memory_space=pltpu.HBM)


def attend_group(queries, fresh, pages, lengths, pool_ref, scores_ref):
    nt = (((1,), (1,)), ((), ()))
    for i in range(GROUP):
        keys = jnp.concatenate([pool_ref[0, page] for page in pages[i]], axis=0)
        scores_ref[i, :, 0:CONTEXT] = lax.dot_general(
            queries[i], keys, nt, preferred_element_type=jnp.float32
        )
        scores_ref[i, :, CONTEXT : CONTEXT + 16] = lax.dot_general(
            queries[i], fresh[i], nt, preferred_element_type=jnp.float32
        )
    outputs = []
    for i in range(GROUP):
        scores = scores_ref[i, :, 0:CONTEXT]
        position = lax.broadcasted_iota(jnp.int32, scores.shape, 1)
        scores = jnp.where(position < lengths[i], scores, NEG_FILL)
        fresh_scores = scores_ref[i, :, CONTEXT : CONTEXT + 16]
        token = lax.broadcasted_iota(jnp.int32, fresh_scores.shape, 1)
        step = lax.broadcasted_iota(jnp.int32, fresh_scores.shape, 0) // 8
        fresh_scores = jnp.where(token <= step, fresh_scores, NEG_FILL)
        highest = jnp.maximum(
            jnp.max(scores, axis=1, keepdims=True), jnp.max(fresh_scores, axis=1, keepdims=True)
        )
        weights = jnp.exp2((scores - highest) * SCALE).astype(jnp.bfloat16)
        fresh_weights = jnp.exp2((fresh_scores - highest) * SCALE).astype(jnp.bfloat16)
        total = jnp.sum(weights.astype(jnp.float32), axis=1, keepdims=True) + jnp.sum(
            fresh_weights.astype(jnp.float32), axis=1, keepdims=True
        )
        values = jnp.concatenate([pool_ref[1, page] for page in pages[i]], axis=0)
        fresh_values = pltpu.roll(fresh[i].astype(jnp.float32), 14, 0).astype(jnp.bfloat16)
        weighted = jnp.dot(weights, values, preferred_element_type=jnp.float32) + jnp.dot(
            fresh_weights, fresh_values, preferred_element_type=jnp.float32
        )
        outputs.append(weighted / total)
    return outputs


def store_rows(out_ref, start, outputs):
    block = jnp.stack(outputs).reshape(16, 8, HEAD).swapaxes(0, 1).astype(jnp.bfloat16)
    for h in range(8):
        out_ref[pl.ds(start, 16), h * HEAD : (h + 1) * HEAD] = block[h]


def fetch_pool(pool_hbm, pool_ref, sem):
    copies = [
        pltpu.make_async_copy(pool_hbm.at[k, p : p + 32], pool_ref.at[k, p : p + 32], sem.at[k, p // 32])
        for k in range(2)
        for p in range(0, 128, 32)
    ]
    for copy in copies:
        copy.start()
    return copies


def stay_kernel(
    table_ref, length_ref, query_ref, fresh_ref, pool_hbm, after_ref, out_ref, pool_ref, scores_ref, sem, *, first
):
    for copy in fetch_pool(pool_hbm, pool_ref, sem):
        copy.wait()

    def group(g, carry):
        rows = [first + g * GROUP + i for i in range(GROUP)]
        outputs = attend_group(
            [query_ref[row] for row in rows],
            [fresh_ref[row] for row in rows],
            [[table_ref[0, row, p] for p in range(PAGES_ROW)] for row in rows],
            [length_ref[0, row] for row in rows],
            pool_ref,
            scores_ref,
        )
        store_rows(out_ref, pl.multiple_of(g * 16, 16), outputs)
        return carry

    lax.fori_loop(0, out_ref.shape[0] // (2 * GROUP), group, 0)


def stay(table, lengths, query, fresh, pool, after, first, count):
    return pl.pallas_call(
        functools.partial(stay_kernel, first=first),
        out_shape=jax.ShapeDtypeStruct((count * 2, 8 * HEAD), jnp.bfloat16),
        in_specs=[SMEM, SMEM, VMEM, VMEM, HBM, SMEM],
        out_specs=VMEM,
        scratch_shapes=[
            pltpu.VMEM(pool.shape, pool.dtype),
            pltpu.VMEM((GROUP, 16, CONTEXT + 128), jnp.float32),
            pltpu.SemaphoreType.DMA((2, 4)),
        ],
        compiler_params=pltpu.CompilerParams(vmem_limit_bytes=24 * 2**20),
        cost_estimate=pl.CostEstimate(flops=count * 10**8, bytes_accessed=8 * 2**20, transcendentals=0),
        name="attend_staying",
    )(table, lengths, query, fresh, pool, after)


def request_kernel(
    offset_ref, order_ref, table_ref, length_ref, query_ref, fresh_ref, out_ref, slot_ref, used
):
    own = lax.axis_index("replica")
    out_ref[...] = jnp.zeros_like(out_ref)
    for s in range(REPLICAS):
        used[s] = 0
    lane = lax.broadcasted_iota(jnp.int32, (1, HEAD), 1)
    line = lax.broadcasted_iota(jnp.int32, (16, HEAD), 0)
    for j in range(MIGRANTS):
        row = STAYING + j
        source = lax.rem(own + 1 + offset_ref[0, j, 0], REPLICAS)
        rank = used[source]
        used[source] = rank + 1
        slot = source * CAP + rank
        slot_ref[j] = slot
        meta = jnp.zeros((1, HEAD), jnp.int32)
        for p in range(PAGES_ROW):
            meta = jnp.where(lane == p, table_ref[0, row, p], meta)
        for c in range(COPIED):
            wanted = table_ref[0, row, order_ref[0, j, c]]
            meta = jnp.where(lane == PAGES_ROW + c, wanted, meta)
        length = length_ref[0, row]
        meta = jnp.where(lane == 20, length // 32, meta)
        meta = jnp.where(lane == 21, lax.rem(length, 32), meta)
        meta = meta.astype(jnp.float32)
        out_ref[slot, 0:16] = query_ref[row]
        out_ref[slot, 16:32] = jnp.where(
            line == META_ROW, meta, fresh_ref[row].astype(jnp.float32)
        ).astype(jnp.bfloat16)


def request(offsets, order, table, lengths, query, fresh):
    return pl.pallas_call(
        request_kernel,
        out_shape=(
            jax.ShapeDtypeStruct((SLOTS, 32, HEAD), jnp.bfloat16),
            jax.ShapeDtypeStruct((MIGRANTS,), jnp.int32),
        ),
        in_specs=[SMEM] * 4 + [VMEM] * 2,
        out_specs=(VMEM, SMEM),
        scratch_shapes=[pltpu.SMEM((REPLICAS,), jnp.int32)],
        name="pack_requests",
    )(offsets, order, table, lengths, query, fresh)


def serve_kernel(
    got_ref, pool_hbm, ret_ref, send_ref, pool_ref, scores_ref, meta_vmem, meta_ref, active, pool_sem, meta_sem, page_sem
):
    fetch = fetch_pool(pool_hbm, pool_ref, pool_sem)
    for slot in range(SLOTS):
        meta_vmem[slot : slot + 1] = got_ref[slot, 16:32].astype(jnp.float32)[META_ROW : META_ROW + 1].astype(jnp.int32)
    meta_copy = pltpu.make_async_copy(meta_vmem, meta_ref, meta_sem)
    meta_copy.start()
    ret_ref[...] = jnp.zeros_like(ret_ref)
    meta_copy.wait()
    for copy in fetch:
        copy.wait()

    def copies(slot, carry):
        for c in range(COPIED):
            page = meta_ref[slot, PAGES_ROW + c]
            pltpu.make_async_copy(pool_ref.at[:, page], send_ref.at[slot, c], page_sem).start()
        return carry

    lax.fori_loop(0, SLOTS, copies, 0)
    for i in range(SLOTS + GROUP):
        active[i] = 0

    def collect(slot, count):
        used = meta_ref[slot, 20] + meta_ref[slot, 21] > 0

        @pl.when(used)
        def _():
            active[count] = slot

        return count + jnp.where(used, 1, 0)

    count = lax.fori_loop(0, SLOTS, collect, 0)

    def group(g, carry):
        slots = [active[g * GROUP + i] for i in range(GROUP)]
        outputs = attend_group(
            [got_ref[slot, 0:16] for slot in slots],
            [got_ref[slot, 16:32] for slot in slots],
            [[meta_ref[slot, p] for p in range(PAGES_ROW)] for slot in slots],
            [meta_ref[slot, 20] * 32 + meta_ref[slot, 21] for slot in slots],
            pool_ref,
            scores_ref,
        )
        for slot, output in zip(slots, outputs):
            ret_ref[slot] = output.astype(jnp.bfloat16)
        return carry

    lax.fori_loop(0, (count + GROUP - 1) // GROUP, group, 0)
    pltpu.make_async_copy(send_ref, send_ref, page_sem).wait()


def serve(got, pool):
    return pl.pallas_call(
        serve_kernel,
        out_shape=(
            jax.ShapeDtypeStruct((SLOTS, 16, HEAD), jnp.bfloat16),
            jax.ShapeDtypeStruct((SLOTS, COPIED, 2, PAGE, HEAD), jnp.bfloat16),
        ),
        in_specs=[VMEM, HBM],
        out_specs=(VMEM, HBM),
        scratch_shapes=[
            pltpu.VMEM(pool.shape, pool.dtype),
            pltpu.VMEM((GROUP, 16, CONTEXT + 128), jnp.float32),
            pltpu.VMEM((SLOTS, HEAD), jnp.int32),
            pltpu.SMEM((SLOTS, HEAD), jnp.int32),
            pltpu.SMEM((SLOTS + GROUP,), jnp.int32),
            pltpu.SemaphoreType.DMA((2, 4)),
            pltpu.SemaphoreType.DMA,
            pltpu.SemaphoreType.DMA,
        ],
        compiler_params=pltpu.CompilerParams(vmem_limit_bytes=24 * 2**20),
        cost_estimate=pl.CostEstimate(flops=4 * 10**9, bytes_accessed=8 * 2**20, transcendentals=0),
        name="serve_requests",
    )(got, pool)


def merge_kernel(slot_ref, first_ref, second_ref, ret_ref, out_ref):
    out_ref[0:128] = first_ref[...]
    out_ref[128:240] = second_ref[...]
    here = [ret_ref[slot_ref[j]].astype(jnp.float32) for j in range(MIGRANTS)]
    store_rows(out_ref, 240, here[6:])
    store_rows(out_ref, 224, here[:2] + here[:6])
    out_ref[224:228] = second_ref[96:100]


def merge(slots, first, second, returned):
    return pl.pallas_call(
        merge_kernel,
        out_shape=jax.ShapeDtypeStruct((ROWS * 2, 8 * HEAD), jnp.bfloat16),
        in_specs=[SMEM, VMEM, VMEM, VMEM],
        out_specs=VMEM,
        name="merge_rows",
    )(slots, first, second, returned)


def pick_kernel(slot_ref, got_ref, out_ref, held, in_sem, out_sem):
    loads = [
        pltpu.make_async_copy(got_ref.at[slot_ref[j]], held.at[j], in_sem.at[j]) for j in range(MIGRANTS)
    ]
    stores = [pltpu.make_async_copy(held.at[j], out_ref.at[j], out_sem.at[j]) for j in range(MIGRANTS)]
    for load in loads:
        load.start()
    for load, store in zip(loads, stores):
        load.wait()
        store.start()
    for store in stores:
        store.wait()


def pick(slots, got):
    shape = (MIGRANTS, COPIED, 2, PAGE, HEAD)
    return pl.pallas_call(
        pick_kernel,
        out_shape=jax.ShapeDtypeStruct(shape, jnp.bfloat16),
        in_specs=[SMEM, HBM],
        out_specs=HBM,
        scratch_shapes=[
            pltpu.VMEM(shape, jnp.bfloat16),
            pltpu.SemaphoreType.DMA((MIGRANTS,)),
            pltpu.SemaphoreType.DMA((MIGRANTS,)),
        ],
        name="pick_pages",
    )(slots, got)


def project_kernel(*refs, starts):
    row_refs, (weight_ref, own_ref, up_ref, far_ref, down_ref, rolled) = refs[:-6], refs[-6:]

    @pl.when(pl.program_id(0) == 0)
    def _():
        zi = lax.axis_index("tensor") // 2
        for z, (which, start) in enumerate(starts):
            place = lax.rem(z - zi + 4, 4) * 32
            rolled[pl.ds(pl.multiple_of(place, 32), 32)] = row_refs[which][start : start + 32]

    product = jnp.dot(rolled[...], weight_ref[...], preferred_element_type=jnp.float32)
    product = product.astype(jnp.bfloat16)
    for k, ref in enumerate((own_ref, up_ref, far_ref, down_ref)):
        ref[...] = product[32 * k : 32 * k + 32]


def project(rows, starts, weight, piece, width):
    tile = 512
    steps = width // tile
    depth = weight.shape[0]
    return pl.pallas_call(
        functools.partial(project_kernel, starts=starts),
        out_shape=[jax.ShapeDtypeStruct((32, width), jnp.bfloat16)] * 4,
        grid=(steps,),
        in_specs=[pl.BlockSpec(r.shape, lambda i: (0, 0)) for r in rows]
        + [pl.BlockSpec((depth, tile), lambda i: (0, piece * steps + i))],
        out_specs=[pl.BlockSpec((32, tile), lambda i: (0, i))] * 4,
        scratch_shapes=[pltpu.VMEM((128, depth), jnp.bfloat16)],
        compiler_params=pltpu.CompilerParams(vmem_limit_bytes=56 * 2**20),
        cost_estimate=pl.CostEstimate(
            flops=2 * 256 * depth * width, bytes_accessed=2 * depth * width, transcendentals=0
        ),
        name="project_piece",
    )(*rows, weight)


def shift_z(value, by):
    pairs = [(z * 2 + x, (z + by) % 4 * 2 + x) for z in range(4) for x in range(2)]
    return lax.ppermute(value, "tensor", pairs)


def send_x(value, to):
    return lax.ppermute(value, "tensor", [(2 * z + 1 - to, 2 * z + to) for z in range(4)])


def f32_sum(*terms):
    return functools.reduce(jnp.add, [term.astype(jnp.float32) for term in terms])


def reduce_z(rows, starts, weight, piece, width):
    here, up, far, down = project(rows, starts, weight, piece, width)
    if piece % 2 == 0:
        up = f32_sum(up, shift_z(far, 1)).astype(jnp.bfloat16)
    else:
        down = f32_sum(down, shift_z(far, -1)).astype(jnp.bfloat16)
    return f32_sum(here, shift_z(up, 1), shift_z(down, -1))


def body(
    queries,
    step_key_value,
    replica_page_store,
    page_table,
    lengths,
    mig_offset,
    copy_order,
    out_weight,
):
    xi = lax.axis_index("tensor") % 2
    pool = replica_page_store[0]
    query = queries[0].reshape(ROWS, 16, HEAD)
    fresh = step_key_value[0]
    fresh = jnp.concatenate(
        [fresh[:, :, 0], fresh[:, :, 1], jnp.zeros((ROWS, 12, HEAD), jnp.bfloat16)], axis=1
    )
    payload, slots = request(mig_offset, copy_order, page_table, lengths, query, fresh)
    got = lax.all_to_all(
        payload.reshape(REPLICAS, CAP, 32, HEAD), "replica", split_axis=0, concat_axis=0, tiled=True
    ).reshape(SLOTS, 32, HEAD)
    first = stay(page_table, lengths, query, fresh, pool, slots, 0, 64)
    answered, sending = serve(got, pool)
    returned = lax.all_to_all(
        answered.reshape(REPLICAS, CAP, 16, HEAD), "replica", split_axis=0, concat_axis=0, tiled=True
    ).reshape(SLOTS, 16, HEAD)
    incoming = lax.all_to_all(
        sending.reshape(REPLICAS, CAP, COPIED, 2, PAGE, HEAD),
        "replica",
        split_axis=0,
        concat_axis=0,
        tiled=True,
    ).reshape(SLOTS, COPIED, 2, PAGE, HEAD)
    second = stay(page_table, lengths, query, fresh, pool, slots, 64, 56)
    merged = merge(slots, first, second, returned)
    width = out_weight.shape[1] // PIECES
    groups = (
        ([first, second], ((0, 0), (0, 64), (1, 0), (1, 64))),
        ([merged], ((0, 32), (0, 96), (0, 160), (0, 224))),
    )
    finished = [[], []]
    for to, (rows, starts) in enumerate(groups):
        for piece in range(PIECES):
            total = reduce_z(rows, starts, out_weight, piece, width)
            finished[to].append(total + send_x(total.astype(jnp.bfloat16), to).astype(jnp.float32))
    projected = jnp.concatenate(
        [jnp.where(xi == 0, zero, one).astype(jnp.bfloat16) for zero, one in zip(*finished)], axis=1
    ).reshape(16, 2, -1)
    arrived = pick(slots, incoming)
    attention = merged.reshape(ROWS, 2, 8 * HEAD)
    return (attention[None], projected[None], arrived[None])


def solution(mesh):
    placed = (
        P("replica", None, None, "tensor"),
        P("replica", None, None, None, "tensor"),
        P("replica", None, None, None, "tensor"),
        P("replica", None, None),
        P("replica", None),
        P("replica", None, None),
        P("replica", None, None),
        P("tensor", None),
    )
    return jax.shard_map(
        body,
        mesh=mesh,
        in_specs=placed,
        out_specs=(
            P("replica", None, None, "tensor"),
            P("replica", "tensor", None, None),
            P("replica", None, None, None, None, "tensor"),
        ),
        check_vma=False,
    )
```

```python
import functools
import math

import jax
import jax.numpy as jnp
from jax import lax
from jax.experimental import pallas as pl
from jax.experimental.pallas import tpu as pltpu
from jax.sharding import PartitionSpec as P

HEAD = 128
ROWS = 128
MIGRANTS = 14
STAYING = ROWS - MIGRANTS
COPIED = 4
PAGES_ROW = 16
PAGE = 64
REPLICAS = 16
CAP = 2
SLOTS = REPLICAS * CAP
GROUP = 8
CONTEXT = PAGES_ROW * PAGE
NEG_FILL = -1e30
SCALE = math.log2(math.e) / math.sqrt(HEAD)
META_ROW = 4
FIRST = 64
WIDTH = 2048
WEIGHT_TILE = 1024
WEIGHT_PARTS = 4
VMEM = pl.BlockSpec(memory_space=pltpu.VMEM)
SMEM = pl.BlockSpec(memory_space=pltpu.SMEM)
HBM = pl.BlockSpec(memory_space=pltpu.HBM)
PARAMS = pltpu.CompilerParams(vmem_limit_bytes=60 * 2**20)


def attend_group(queries, fresh, pages, lengths, pool_ref, scores_ref):
    nt = (((1,), (1,)), ((), ()))
    for i in range(GROUP):
        keys = jnp.concatenate([pool_ref[0, page] for page in pages[i]], axis=0)
        scores_ref[i, :, 0:CONTEXT] = lax.dot_general(
            queries[i], keys, nt, preferred_element_type=jnp.float32
        )
        scores_ref[i, :, CONTEXT : CONTEXT + 8] = lax.dot_general(
            queries[i], fresh[i].astype(jnp.bfloat16), nt, preferred_element_type=jnp.float32
        )
    outputs = []
    for i in range(GROUP):
        scores = scores_ref[i, :, 0:CONTEXT]
        position = lax.broadcasted_iota(jnp.int32, scores.shape, 1)
        scores = jnp.where(position < lengths[i], scores, NEG_FILL)
        fresh_scores = scores_ref[i, :, CONTEXT : CONTEXT + 8]
        line = lax.broadcasted_iota(jnp.int32, fresh_scores.shape, 1)
        step = lax.rem(lax.broadcasted_iota(jnp.int32, fresh_scores.shape, 0), 2)
        fresh_scores = jnp.where((line == 0) | (line == 2 * step), fresh_scores, NEG_FILL)
        highest = jnp.maximum(
            jnp.max(scores, axis=1, keepdims=True), jnp.max(fresh_scores, axis=1, keepdims=True)
        )
        weights = jnp.exp2((scores - highest) * SCALE).astype(jnp.bfloat16)
        fresh_weights = jnp.exp2((fresh_scores - highest) * SCALE).astype(jnp.bfloat16)
        total = jnp.sum(weights.astype(jnp.float32), axis=1, keepdims=True) + jnp.sum(
            fresh_weights.astype(jnp.float32), axis=1, keepdims=True
        )
        values = jnp.concatenate([pool_ref[1, page] for page in pages[i]], axis=0)
        fresh_values = pltpu.roll(fresh[i], 7, 0).astype(jnp.bfloat16)
        weighted = jnp.dot(weights, values, preferred_element_type=jnp.float32) + jnp.dot(
            fresh_weights, fresh_values, preferred_element_type=jnp.float32
        )
        outputs.append((weighted / total).astype(jnp.bfloat16))
    return outputs


def fresh_rows(tokens):
    tokens = tokens.astype(jnp.float32).reshape(4, HEAD)
    return jnp.concatenate([tokens, jnp.zeros((4, HEAD), jnp.float32)], axis=0)


def fetch_pool(pool_hbm, pool_ref, sem):
    copies = [
        pltpu.make_async_copy(pool_hbm.at[k, p : p + 32], pool_ref.at[k, p : p + 32], sem.at[k, p // 32])
        for k in range(2)
        for p in range(0, 128, 32)
    ]
    for copy in copies:
        copy.start()
    return copies


def attend_staying(table_ref, length_ref, query_ref, fresh_ref, out_ref, pool_ref, scores_ref, first):
    def group(g, carry):
        rows = [first + g * GROUP + i for i in range(GROUP)]
        outputs = attend_group(
            [query_ref[row].reshape(16, HEAD) for row in rows],
            [fresh_rows(fresh_ref[row]) for row in rows],
            [[table_ref[p, row] for p in range(PAGES_ROW)] for row in rows],
            [length_ref[0, row] for row in rows],
            pool_ref,
            scores_ref,
        )
        for i, output in enumerate(outputs):
            out_ref[g * GROUP + i] = output.reshape(8, 2, HEAD)
        return carry

    lax.fori_loop(0, out_ref.shape[0] // GROUP, group, 0)


def stay_kernel(table_ref, length_ref, query_ref, fresh_ref, pool_hbm, out_ref, pool_ref, scores_ref, sem):
    for copy in fetch_pool(pool_hbm, pool_ref, sem):
        copy.wait()
    attend_staying(table_ref, length_ref, query_ref, fresh_ref, out_ref, pool_ref, scores_ref, 0)


def attention_scratch(pool):
    return [
        pltpu.VMEM(pool.shape, pool.dtype),
        pltpu.VMEM((GROUP, 16, CONTEXT + 128), jnp.float32),
        pltpu.SemaphoreType.DMA((2, 4)),
    ]


def stay(table, lengths, query, fresh, pool, count):
    return pl.pallas_call(
        stay_kernel,
        out_shape=jax.ShapeDtypeStruct((count, 8, 2, HEAD), jnp.bfloat16),
        in_specs=[SMEM, SMEM, VMEM, VMEM, HBM],
        out_specs=VMEM,
        scratch_shapes=attention_scratch(pool),
        compiler_params=PARAMS,
        cost_estimate=pl.CostEstimate(flops=8 * 10**9, bytes_accessed=8 * 2**20, transcendentals=0),
        name="attend_first",
    )(table, lengths, query, fresh, pool)


def fetch_weight(weight_hbm, weight_ref, sem, start):
    copies = []
    for c in range(WEIGHT_PARTS):
        place = c * WEIGHT_TILE
        copies.append(
            pltpu.make_async_copy(
                weight_hbm.at[:, start + place : start + place + WEIGHT_TILE],
                weight_ref.at[:, place : place + WEIGHT_TILE],
                sem.at[c],
            )
        )
    for copy in copies:
        copy.start()
    return copies


def second_kernel(
    meta_ref, table_ref, length_ref, query_ref, fresh_ref, pool_hbm, out_ref, send_ref, pool_ref, scores_ref, sem, page_sem
):
    for copy in fetch_pool(pool_hbm, pool_ref, sem):
        copy.wait()

    def copies(slot, carry):
        for c in range(COPIED):
            page = meta_ref[slot, PAGES_ROW + c]
            pltpu.make_async_copy(pool_ref.at[:, page], send_ref.at[slot, c], page_sem).start()
        return carry

    lax.fori_loop(0, SLOTS, copies, 0)
    attend_staying(table_ref, length_ref, query_ref, fresh_ref, out_ref, pool_ref, scores_ref, FIRST)
    pltpu.make_async_copy(send_ref, send_ref, page_sem).wait()


def attend_second(meta, table, lengths, query, fresh, pool):
    return pl.pallas_call(
        second_kernel,
        out_shape=(
            jax.ShapeDtypeStruct((120 - FIRST, 8, 2, HEAD), jnp.bfloat16),
            jax.ShapeDtypeStruct((SLOTS, COPIED, 2, PAGE, HEAD), jnp.bfloat16),
        ),
        in_specs=[SMEM, SMEM, SMEM, VMEM, VMEM, HBM],
        out_specs=(VMEM, HBM),
        scratch_shapes=attention_scratch(pool) + [pltpu.SemaphoreType.DMA],
        compiler_params=PARAMS,
        cost_estimate=pl.CostEstimate(flops=8 * 10**9, bytes_accessed=8 * 2**20, transcendentals=0),
        name="attend_second",
    )(meta, table, lengths, query, fresh, pool)


def project_rolled(rolled_ref, weight_ref, fetch, part_refs):
    for c, copy in enumerate(fetch):
        copy.wait()
        product = jnp.dot(
            rolled_ref[...],
            weight_ref[:, c * WEIGHT_TILE : (c + 1) * WEIGHT_TILE],
            preferred_element_type=jnp.float32,
        ).astype(jnp.bfloat16)
        piece, place = divmod(c * WEIGHT_TILE, WIDTH)
        for k in range(4):
            part_refs[piece * 4 + k][:, place : place + WEIGHT_TILE] = product[64 * k : 64 * k + 64]


PARTS = [jax.ShapeDtypeStruct((64, WIDTH), jnp.bfloat16)] * 8


def weight_scratch(weight):
    return [pltpu.VMEM((weight.shape[0], 2 * WIDTH), weight.dtype), pltpu.SemaphoreType.DMA((WEIGHT_PARTS,))]


def merge_kernel(place_ref, first_ref, second_ref, ret_ref, weight_hbm, out_ref, rolled_ref, *refs):
    part_refs, (weight_ref, weight_sem) = refs[:8], refs[8:]
    fetch = fetch_weight(weight_hbm, weight_ref, weight_sem, 0)
    out_ref[0:FIRST] = first_ref[...]
    out_ref[FIRST:STAYING] = second_ref[0 : STAYING - FIRST]
    for j in range(MIGRANTS):
        out_ref[STAYING + j] = ret_ref[place_ref[j]].reshape(8, 2, HEAD)
    zi = lax.axis_index("tensor") // 2
    for z in range(4):
        place = pl.multiple_of(lax.rem(z - zi + 4, 4) * 64, 64)
        for h in range(8):
            rolled_ref[pl.ds(place, 64), h * HEAD : (h + 1) * HEAD] = out_ref[32 * z : 32 * z + 32, h].reshape(64, HEAD)
    project_rolled(rolled_ref, weight_ref, fetch, part_refs)


def merge_project(places, first, second, returned, weight):
    out = pl.pallas_call(
        merge_kernel,
        out_shape=[
            jax.ShapeDtypeStruct((ROWS, 8, 2, HEAD), jnp.bfloat16),
            jax.ShapeDtypeStruct((2 * ROWS, 8 * HEAD), jnp.bfloat16),
        ]
        + PARTS,
        in_specs=[SMEM, VMEM, VMEM, VMEM, HBM],
        out_specs=[VMEM] * 10,
        scratch_shapes=weight_scratch(weight),
        compiler_params=PARAMS,
        cost_estimate=pl.CostEstimate(flops=5 * 10**9, bytes_accessed=8 * 2**20, transcendentals=0),
        name="merge_project",
    )(places, first, second, returned, weight)
    return out[0], out[1], out[2:]


def project_kernel(rolled_ref, weight_hbm, *refs):
    part_refs, (weight_ref, weight_sem) = refs[:8], refs[8:]
    project_rolled(rolled_ref, weight_ref, fetch_weight(weight_hbm, weight_ref, weight_sem, 2 * WIDTH), part_refs)


def project(rolled, weight):
    return pl.pallas_call(
        project_kernel,
        out_shape=PARTS,
        in_specs=[VMEM, HBM],
        out_specs=[VMEM] * 8,
        scratch_shapes=weight_scratch(weight),
        compiler_params=PARAMS,
        cost_estimate=pl.CostEstimate(flops=5 * 10**9, bytes_accessed=8 * 2**20, transcendentals=0),
        name="project_rest",
    )(rolled, weight)


def request_kernel(
    offset_ref, order_ref, table_ref, length_ref, query_ref, fresh_ref, out_ref, slot_ref, used
):
    own = lax.axis_index("replica")
    out_ref[...] = jnp.zeros_like(out_ref)
    for s in range(REPLICAS):
        used[s] = 0
    lane = lax.broadcasted_iota(jnp.int32, (1, HEAD), 1)
    for j in range(MIGRANTS):
        row = STAYING + j
        source = lax.rem(own + 1 + offset_ref[0, j], REPLICAS)
        rank = used[source]
        used[source] = rank + 1
        slot = source * CAP + rank
        slot_ref[j] = slot
        meta = jnp.zeros((1, HEAD), jnp.int32)
        for p in range(PAGES_ROW):
            meta = jnp.where(lane == p, table_ref[p, row], meta)
        for c in range(COPIED):
            wanted = table_ref[order_ref[j, 0, c], row]
            meta = jnp.where(lane == PAGES_ROW + c, wanted, meta)
        length = length_ref[0, row]
        meta = jnp.where(lane == 20, length // 32, meta)
        meta = jnp.where(lane == 21, lax.rem(length, 32), meta)
        out_ref[slot, 0:16] = query_ref[row].reshape(16, HEAD)
        out_ref[slot, 16:32] = jnp.concatenate(
            [
                fresh_ref[row].astype(jnp.float32).reshape(4, HEAD),
                meta.astype(jnp.float32),
                jnp.zeros((11, HEAD), jnp.float32),
            ],
            axis=0,
        ).astype(jnp.bfloat16)


def request(offsets, order, table, lengths, query, fresh):
    return pl.pallas_call(
        request_kernel,
        out_shape=(
            jax.ShapeDtypeStruct((SLOTS, 32, HEAD), jnp.bfloat16),
            jax.ShapeDtypeStruct((MIGRANTS,), jnp.int32),
        ),
        in_specs=[SMEM] * 4 + [VMEM] * 2,
        out_specs=(VMEM, SMEM),
        scratch_shapes=[pltpu.SMEM((REPLICAS,), jnp.int32)],
        compiler_params=PARAMS,
        name="pack_requests",
    )(offsets, order, table, lengths, query, fresh)


def serve_kernel(
    got_ref, after_ref, pool_hbm, ret_ref, meta_ref, pool_ref, scores_ref, pool_sem, meta_vmem, active, meta_sem
):
    fetch = fetch_pool(pool_hbm, pool_ref, pool_sem)
    for slot in range(SLOTS):
        meta_vmem[slot : slot + 1] = got_ref[slot, 16:32].astype(jnp.float32)[META_ROW : META_ROW + 1].astype(jnp.int32)
    meta_copy = pltpu.make_async_copy(meta_vmem, meta_ref, meta_sem)
    meta_copy.start()
    ret_ref[...] = jnp.zeros_like(ret_ref)
    for i in range(SLOTS + GROUP):
        active[i] = 0
    meta_copy.wait()

    def collect(slot, count):
        used = meta_ref[slot, 20] + meta_ref[slot, 21] > 0

        @pl.when(used)
        def _():
            active[count] = slot

        return count + jnp.where(used, 1, 0)

    count = lax.fori_loop(0, SLOTS, collect, 0)
    for copy in fetch:
        copy.wait()

    def group(g, carry):
        slots = [active[g * GROUP + i] for i in range(GROUP)]
        outputs = attend_group(
            [got_ref[slot, 0:16] for slot in slots],
            [got_ref[slot, 16:32].astype(jnp.float32)[0:8] for slot in slots],
            [[meta_ref[slot, p] for p in range(PAGES_ROW)] for slot in slots],
            [meta_ref[slot, 20] * 32 + meta_ref[slot, 21] for slot in slots],
            pool_ref,
            scores_ref,
        )
        for slot, output in zip(slots, outputs):
            ret_ref[slot] = output
        return carry

    lax.fori_loop(0, (count + GROUP - 1) // GROUP, group, 0)


def serve(got, after, pool):
    return pl.pallas_call(
        serve_kernel,
        out_shape=(
            jax.ShapeDtypeStruct((SLOTS, 16, HEAD), jnp.bfloat16),
            jax.ShapeDtypeStruct((SLOTS, HEAD), jnp.int32),
        ),
        in_specs=[VMEM, HBM, HBM],
        out_specs=(VMEM, SMEM),
        scratch_shapes=attention_scratch(pool)
        + [
            pltpu.VMEM((SLOTS, HEAD), jnp.int32),
            pltpu.SMEM((SLOTS + GROUP,), jnp.int32),
            pltpu.SemaphoreType.DMA,
        ],
        compiler_params=PARAMS,
        cost_estimate=pl.CostEstimate(flops=6 * 10**9, bytes_accessed=8 * 2**20, transcendentals=0),
        name="serve_requests",
    )(got, after, pool)


def pick_kernel(slot_ref, got_ref, out_ref, held, in_sem, out_sem):
    loads = [
        pltpu.make_async_copy(got_ref.at[slot_ref[j]], held.at[j], in_sem.at[j]) for j in range(MIGRANTS)
    ]
    stores = [pltpu.make_async_copy(held.at[j], out_ref.at[j], out_sem.at[j]) for j in range(MIGRANTS)]
    for load in loads:
        load.start()
    for load, store in zip(loads, stores):
        load.wait()
        store.start()
    for store in stores:
        store.wait()


def pick(slots, got):
    shape = (MIGRANTS, COPIED, 2, PAGE, HEAD)
    return pl.pallas_call(
        pick_kernel,
        out_shape=jax.ShapeDtypeStruct(shape, jnp.bfloat16),
        in_specs=[SMEM, HBM],
        out_specs=HBM,
        scratch_shapes=[
            pltpu.VMEM(shape, jnp.bfloat16),
            pltpu.SemaphoreType.DMA((MIGRANTS,)),
            pltpu.SemaphoreType.DMA((MIGRANTS,)),
        ],
        compiler_params=PARAMS,
        name="pick_pages",
    )(slots, got)


def shift_z(value, by):
    pairs = [(z * 2 + x, (z + by) % 4 * 2 + x) for z in range(4) for x in range(2)]
    return lax.ppermute(value, "tensor", pairs)


def swap_x(value):
    return lax.ppermute(value, "tensor", [(t, t ^ 1) for t in range(8)])


def f32_sum(*terms):
    return functools.reduce(jnp.add, [term.astype(jnp.float32) for term in terms])


def reduce_z(here, up, far, down, piece):
    if piece == 0:
        up = f32_sum(up, shift_z(far, 1)).astype(jnp.bfloat16)
    else:
        down = f32_sum(down, shift_z(far, -1)).astype(jnp.bfloat16)
    return f32_sum(here, shift_z(up, 1), shift_z(down, -1))


def body(
    queries,
    step_key_value,
    replica_page_store,
    page_table,
    lengths,
    mig_offset,
    copy_order,
    out_weight,
):
    xi = lax.axis_index("tensor") % 2
    pool = replica_page_store[0]
    query = queries[0].reshape(ROWS, 2, 8, HEAD).transpose(0, 2, 1, 3)
    fresh = step_key_value[0]
    table = page_table[0].T
    payload, slots = request(
        mig_offset[:, :, 0], copy_order.transpose(1, 0, 2), table, lengths, query, fresh
    )
    got = lax.all_to_all(
        payload.reshape(REPLICAS, CAP, 32, HEAD), "replica", split_axis=0, concat_axis=0, tiled=True
    ).reshape(SLOTS, 32, HEAD)
    first = stay(table, lengths, query, fresh, pool, FIRST)
    answered, meta = serve(got, first, pool)
    returned = lax.all_to_all(
        answered.reshape(REPLICAS, CAP, 16, HEAD), "replica", split_axis=0, concat_axis=0, tiled=True
    ).reshape(SLOTS, 16, HEAD)
    second, sending = attend_second(meta, table, lengths, query, fresh, pool)
    incoming = lax.all_to_all(
        sending.reshape(REPLICAS, CAP, COPIED, 2, PAGE, HEAD),
        "replica",
        split_axis=0,
        concat_axis=0,
        tiled=True,
    ).reshape(SLOTS, COPIED, 2, PAGE, HEAD)
    merged, rolled, parts = merge_project(slots, first, second, returned, out_weight)
    parts = list(parts) + list(project(rolled, out_weight))
    finished = []
    for piece in range(4):
        total = reduce_z(*parts[piece * 4 : piece * 4 + 4], piece % 2).reshape(2, 32, WIDTH)
        mine = lax.dynamic_index_in_dim(total, xi, 0, keepdims=False)
        other = lax.dynamic_index_in_dim(total, 1 - xi, 0, keepdims=False)
        finished.append((mine + swap_x(other.astype(jnp.bfloat16)).astype(jnp.float32)).astype(jnp.bfloat16))
    projected = jnp.concatenate(finished, axis=1).reshape(16, 2, -1)
    arrived = pick(slots, incoming)
    attention = merged.transpose(0, 2, 1, 3).reshape(ROWS, 2, 8 * HEAD)
    return (attention[None], projected[None], arrived[None])


def solution(mesh):
    placed = (
        P("replica", None, None, "tensor"),
        P("replica", None, None, None, "tensor"),
        P("replica", None, None, None, "tensor"),
        P("replica", None, None),
        P("replica", None),
        P("replica", None, None),
        P("replica", None, None),
        P("tensor", None),
    )
    return jax.shard_map(
        body,
        mesh=mesh,
        in_specs=placed,
        out_specs=(
            P("replica", None, None, "tensor"),
            P("replica", "tensor", None, None),
            P("replica", None, None, None, None, "tensor"),
        ),
        check_vma=False,
    )
```

```python
import functools
import math

import jax
import jax.numpy as jnp
from jax import lax
from jax.experimental import pallas as pl
from jax.experimental.pallas import tpu as pltpu
from jax.sharding import PartitionSpec as P

HEAD = 128
ROWS = 128
MIGRANTS = 14
STAYING = ROWS - MIGRANTS
COPIED = 4
PAGES_ROW = 16
PAGE = 64
REPLICAS = 16
CAP = 2
SLOTS = REPLICAS * CAP
GROUP = 8
CONTEXT = PAGES_ROW * PAGE
NEG_FILL = -1e30
SCALE = math.log2(math.e) / math.sqrt(HEAD)
META_ROW = 4
CHUNK = 256
FIRST = 48
SECOND = 32
THIRD = 40
WIDTH = 2048
WEIGHT_TILE = 1024
WEIGHT_PARTS = 8
VMEM = pl.BlockSpec(memory_space=pltpu.VMEM)
SMEM = pl.BlockSpec(memory_space=pltpu.SMEM)
HBM = pl.BlockSpec(memory_space=pltpu.HBM)
PARAMS = pltpu.CompilerParams(vmem_limit_bytes=60 * 2**20)


def attend_group(tokens, queries, fresh, pages, lengths, pool_ref, scores_ref):
    nt = (((1,), (1,)), ((), ()))
    for i in range(GROUP):
        keys = jnp.concatenate([pool_ref[0, page] for page in pages[i][: tokens // PAGE]], axis=0)
        scores_ref[i, :, 0:tokens] = lax.dot_general(
            queries[i], keys, nt, preferred_element_type=jnp.float32
        )
        scores_ref[i, :, CONTEXT : CONTEXT + 8] = lax.dot_general(
            queries[i], fresh[i].astype(jnp.bfloat16), nt, preferred_element_type=jnp.float32
        )
    outputs = []
    for i in range(GROUP):
        scores = scores_ref[i, :, 0:tokens]
        position = lax.broadcasted_iota(jnp.int32, scores.shape, 1)
        scores = jnp.where(position < lengths[i], scores, NEG_FILL)
        fresh_scores = scores_ref[i, :, CONTEXT : CONTEXT + 8]
        line = lax.broadcasted_iota(jnp.int32, fresh_scores.shape, 1)
        step = lax.rem(lax.broadcasted_iota(jnp.int32, fresh_scores.shape, 0), 2)
        fresh_scores = jnp.where((line == 0) | (line == 2 * step), fresh_scores, NEG_FILL)
        highest = jnp.maximum(
            jnp.max(scores, axis=1, keepdims=True), jnp.max(fresh_scores, axis=1, keepdims=True)
        )
        weights = jnp.exp2((scores - highest) * SCALE).astype(jnp.bfloat16)
        fresh_weights = jnp.exp2((fresh_scores - highest) * SCALE).astype(jnp.bfloat16)
        total = jnp.sum(weights.astype(jnp.float32), axis=1, keepdims=True) + jnp.sum(
            fresh_weights.astype(jnp.float32), axis=1, keepdims=True
        )
        values = jnp.concatenate([pool_ref[1, page] for page in pages[i][: tokens // PAGE]], axis=0)
        fresh_values = pltpu.roll(fresh[i], 7, 0).astype(jnp.bfloat16)
        weighted = jnp.dot(weights, values, preferred_element_type=jnp.float32) + jnp.dot(
            fresh_weights, fresh_values, preferred_element_type=jnp.float32
        )
        outputs.append((weighted / total).astype(jnp.bfloat16))
    return outputs


def fresh_rows(tokens):
    tokens = tokens.astype(jnp.float32).reshape(4, HEAD)
    return jnp.concatenate([tokens, jnp.zeros((4, HEAD), jnp.float32)], axis=0)


def fetch_pool(pool_hbm, pool_ref, sem):
    copies = [
        pltpu.make_async_copy(pool_hbm.at[k, p : p + 32], pool_ref.at[k, p : p + 32], sem.at[k, p // 32])
        for k in range(2)
        for p in range(0, 128, 32)
    ]
    for copy in copies:
        copy.start()
    return copies


def chunks_of(length):
    return (length + CHUNK - 1) // CHUNK


def sort_rows(length_of, count, order_ref):
    def tally(i, counts):
        chunks = chunks_of(length_of(i))
        return tuple(c + jnp.where(chunks == k, 1, 0) for k, c in enumerate(counts))

    zero = jnp.int32(0)
    counts = lax.fori_loop(0, count, tally, (zero,) * 5)
    starts = [zero]
    for c in counts[:4]:
        starts.append(starts[-1] + c)

    def put(i, starts):
        chunks = chunks_of(length_of(i))
        place = zero
        for k in range(5):
            place = jnp.where(chunks == k, starts[k], place)
        order_ref[place] = i
        return tuple(s + jnp.where(chunks == k, 1, 0) for k, s in enumerate(starts))

    lax.fori_loop(0, count, put, tuple(starts))
    return counts[0]


def each_group(groups, order_ref, length_of, attend):
    def group(g, carry):
        rows = [order_ref[g * GROUP + i] for i in range(GROUP)]
        chunks = jnp.maximum(chunks_of(length_of(rows[-1])), 1)
        for k in range(1, CONTEXT // CHUNK + 1):

            @pl.when(chunks == k)
            def _():
                attend(k * CHUNK, rows)

        return carry

    lax.fori_loop(groups[0], groups[1], group, 0)


def stay_copies(first, count, query_hbm, fresh_hbm, query_ref, fresh_ref, sem):
    copies = [
        pltpu.make_async_copy(query_hbm.at[first : first + count], query_ref, sem.at[0]),
        pltpu.make_async_copy(fresh_hbm.at[first : first + count], fresh_ref, sem.at[1]),
    ]
    for copy in copies:
        copy.start()
    return copies


def attend_staying(
    first, count, table_ref, length_ref, query_hbm, fresh_hbm, pool_hbm, out_ref, out_first, refs, meanwhile=None
):
    pool_ref, scores_ref, pool_sem, query_ref, fresh_ref, order_ref, row_sem = refs
    copies = fetch_pool(pool_hbm, pool_ref, pool_sem)
    copies += stay_copies(first, count, query_hbm, fresh_hbm, query_ref, fresh_ref, row_sem)
    length_of = lambda i: jnp.where(first + i < STAYING, length_ref[0, first + i], 1)
    sort_rows(length_of, count, order_ref)
    for copy in copies:
        copy.wait()
    started = meanwhile() if meanwhile is not None else None

    def attend(tokens, rows):
        outputs = attend_group(
            tokens,
            [query_ref[row].reshape(16, HEAD) for row in rows],
            [fresh_rows(fresh_ref[row]) for row in rows],
            [[table_ref[p, first + row] for p in range(PAGES_ROW)] for row in rows],
            [length_of(row) for row in rows],
            pool_ref,
            scores_ref,
        )
        for row, output in zip(rows, outputs):
            out_ref[out_first + row] = output.reshape(8, 2, HEAD)

    each_group((0, count // GROUP), order_ref, length_of, attend)
    return started


def stay_kernel(table_ref, length_ref, query_hbm, fresh_hbm, pool_hbm, out_ref, *refs):
    attend_staying(0, FIRST, table_ref, length_ref, query_hbm, fresh_hbm, pool_hbm, out_ref, 0, refs)


def attention_scratch(pool):
    return [
        pltpu.VMEM(pool.shape, pool.dtype),
        pltpu.VMEM((GROUP, 16, CONTEXT + 128), jnp.float32),
        pltpu.SemaphoreType.DMA((2, 4)),
    ]


def stay_scratch(pool, count):
    return attention_scratch(pool) + [
        pltpu.VMEM((count, 8, 2, HEAD), jnp.bfloat16),
        pltpu.VMEM((count, 2, 2, HEAD), jnp.bfloat16),
        pltpu.SMEM((count,), jnp.int32),
        pltpu.SemaphoreType.DMA((2,)),
    ]


def stay(table, lengths, query, fresh, pool, count):
    return pl.pallas_call(
        stay_kernel,
        out_shape=jax.ShapeDtypeStruct((count, 8, 2, HEAD), jnp.bfloat16),
        in_specs=[SMEM, SMEM, HBM, HBM, HBM],
        out_specs=VMEM,
        scratch_shapes=stay_scratch(pool, count),
        compiler_params=PARAMS,
        cost_estimate=pl.CostEstimate(flops=8 * 10**9, bytes_accessed=8 * 2**20, transcendentals=0),
        name="attend_first",
    )(table, lengths, query, fresh, pool)


def fetch_weight(weight_hbm, weight_ref, sem):
    copies = []
    for c in range(WEIGHT_PARTS):
        columns = slice(c * WEIGHT_TILE, (c + 1) * WEIGHT_TILE)
        copies.append(pltpu.make_async_copy(weight_hbm.at[:, columns], weight_ref.at[:, columns], sem.at[c]))
    for copy in copies:
        copy.start()
    return copies


def second_kernel(after_ref, table_ref, length_ref, query_hbm, fresh_hbm, pool_hbm, out_ref, *refs):
    attend_staying(FIRST, SECOND, table_ref, length_ref, query_hbm, fresh_hbm, pool_hbm, out_ref, 0, refs)


def attend_second(after, table, lengths, query, fresh, pool):
    return pl.pallas_call(
        second_kernel,
        out_shape=jax.ShapeDtypeStruct((SECOND, 8, 2, HEAD), jnp.bfloat16),
        in_specs=[SMEM, SMEM, SMEM, HBM, HBM, HBM],
        out_specs=VMEM,
        scratch_shapes=stay_scratch(pool, SECOND),
        compiler_params=PARAMS,
        cost_estimate=pl.CostEstimate(flops=8 * 10**9, bytes_accessed=8 * 2**20, transcendentals=0),
        name="attend_second",
    )(after, table, lengths, query, fresh, pool)


def project_rolled(rolled_ref, weight_ref, fetch, held_refs, part_refs, sem):
    copies = []
    for c, copy in enumerate(fetch):
        copy.wait()
        start = c * WEIGHT_TILE
        product = jnp.dot(
            rolled_ref[...], weight_ref[:, start : start + WEIGHT_TILE], preferred_element_type=jnp.float32
        ).astype(jnp.bfloat16)
        half, start = divmod(start, 2 * WIDTH)
        own, above, far, below = (product[64 * k : 64 * k + 64] for k in range(4))
        place = slice(start % WIDTH, start % WIDTH + WEIGHT_TILE)
        first, second = slice(0, 64), slice(64, 128)
        if start < WIDTH:
            puts = [(1, first, far), (2, second, below), (3, first, above)]
        else:
            puts = [(2, first, far), (1, second, above), (4, first, below)]
        puts = [(part, lines, place, value) for part, lines, value in puts]
        puts.append((0, first, slice(start, start + WEIGHT_TILE), own))
        for k, (part, lines, columns, value) in enumerate(puts):
            held, target = held_refs[half * 5 + part], part_refs[half * 5 + part]
            held[lines, columns] = value
            copies.append(pltpu.make_async_copy(held.at[lines, columns], target.at[lines, columns], sem.at[c, k]))
            copies[-1].start()
    return copies


PART_SHAPES = ((64, 2 * WIDTH), (128, WIDTH), (128, WIDTH), (64, WIDTH), (64, WIDTH)) * 2


def project_kernel(
    slot_ref, table_ref, length_ref, query_hbm, fresh_hbm, pool_hbm, first_ref, second_ref, ret_ref, weight_hbm,
    out_ref, *refs
):
    part_refs, refs = refs[:10], refs[10:]
    stay_refs, held_refs, (weight_ref, rolled_ref, weight_sem, part_sem) = refs[:-14], refs[-14:-4], refs[-4:]
    done = FIRST + SECOND

    def start_weight():
        return fetch_weight(weight_hbm, weight_ref, weight_sem)

    fetch = attend_staying(
        done, THIRD, table_ref, length_ref, query_hbm, fresh_hbm, pool_hbm, out_ref, done, stay_refs, start_weight
    )
    out_ref[0:FIRST] = first_ref[...]
    out_ref[FIRST:done] = second_ref[...]
    for j in range(MIGRANTS):
        out_ref[STAYING + j] = ret_ref[slot_ref[j]].reshape(8, 2, HEAD)
    zi = lax.axis_index("tensor") // 2
    for z in range(4):
        place = pl.multiple_of(lax.rem(z - zi + 4, 4) * 64, 64)
        for h in range(8):
            rolled_ref[pl.ds(place, 64), h * HEAD : (h + 1) * HEAD] = out_ref[32 * z : 32 * z + 32, h].reshape(64, HEAD)
    for copy in project_rolled(rolled_ref, weight_ref, fetch, held_refs, part_refs, part_sem):
        copy.wait()


def project(slots, table, lengths, query, fresh, pool, first, second, returned, weight):
    out = pl.pallas_call(
        project_kernel,
        out_shape=[jax.ShapeDtypeStruct((ROWS, 8, 2, HEAD), jnp.bfloat16)]
        + [jax.ShapeDtypeStruct(shape, jnp.bfloat16) for shape in PART_SHAPES],
        in_specs=[SMEM, SMEM, SMEM, HBM, HBM, HBM, VMEM, VMEM, VMEM, HBM],
        out_specs=[VMEM] + [HBM] * 10,
        scratch_shapes=stay_scratch(pool, THIRD)
        + [pltpu.VMEM(shape, jnp.bfloat16) for shape in PART_SHAPES]
        + [
            pltpu.VMEM(weight.shape, weight.dtype),
            pltpu.VMEM((2 * ROWS, weight.shape[0]), jnp.bfloat16),
            pltpu.SemaphoreType.DMA((WEIGHT_PARTS,)),
            pltpu.SemaphoreType.DMA((WEIGHT_PARTS, 4)),
        ],
        compiler_params=PARAMS,
        cost_estimate=pl.CostEstimate(flops=10**9, bytes_accessed=2**20, transcendentals=0),
        name="attend_third_project",
    )(slots, table, lengths, query, fresh, pool, first, second, returned, weight)
    return out[0], list(out[1:6]), list(out[6:])


def same_kernel(*refs):
    pass


def second_turn(up, down):
    return pl.pallas_call(
        same_kernel,
        out_shape=[jax.ShapeDtypeStruct(x.shape, x.dtype) for x in (up, down)],
        in_specs=[HBM, HBM],
        out_specs=[HBM, HBM],
        input_output_aliases={0: 0, 1: 1},
        compiler_params=PARAMS,
        cost_estimate=pl.CostEstimate(flops=3 * 10**10, bytes_accessed=2**20, transcendentals=0),
        name="second_turn",
    )(up, down)


def request_kernel(
    offset_ref, order_ref, table_ref, length_ref, query_ref, fresh_ref, out_ref, slot_ref, used
):
    own = lax.axis_index("replica")
    out_ref[...] = jnp.zeros_like(out_ref)
    for s in range(REPLICAS):
        used[s] = 0
    lane = lax.broadcasted_iota(jnp.int32, (1, HEAD), 1)
    for j in range(MIGRANTS):
        row = STAYING + j
        source = lax.rem(own + 1 + offset_ref[0, j], REPLICAS)
        rank = used[source]
        used[source] = rank + 1
        slot = source * CAP + rank
        slot_ref[j] = slot
        meta = jnp.zeros((1, HEAD), jnp.int32)
        for p in range(PAGES_ROW):
            meta = jnp.where(lane == p, table_ref[p, row], meta)
        for c in range(COPIED):
            wanted = table_ref[order_ref[j, 0, c], row]
            meta = jnp.where(lane == PAGES_ROW + c, wanted, meta)
        length = length_ref[0, row]
        meta = jnp.where(lane == 20, length // 32, meta)
        meta = jnp.where(lane == 21, lax.rem(length, 32), meta)
        out_ref[slot, 0:16] = query_ref[row].reshape(16, HEAD)
        out_ref[slot, 16:32] = jnp.concatenate(
            [
                fresh_ref[row].astype(jnp.float32).reshape(4, HEAD),
                meta.astype(jnp.float32),
                jnp.zeros((11, HEAD), jnp.float32),
            ],
            axis=0,
        ).astype(jnp.bfloat16)


def request(offsets, order, table, lengths, query, fresh):
    return pl.pallas_call(
        request_kernel,
        out_shape=(
            jax.ShapeDtypeStruct((SLOTS, 32, HEAD), jnp.bfloat16),
            jax.ShapeDtypeStruct((MIGRANTS,), jnp.int32),
        ),
        in_specs=[SMEM] * 4 + [VMEM] * 2,
        out_specs=(VMEM, SMEM),
        scratch_shapes=[pltpu.SMEM((REPLICAS,), jnp.int32)],
        compiler_params=PARAMS,
        name="pack_requests",
    )(offsets, order, table, lengths, query, fresh)


def serve_kernel(
    got_ref, after_ref, pool_hbm, ret_ref, send_ref, unused_ref, pool_ref, scores_ref, pool_sem, meta_vmem, meta_ref, order_ref,
    meta_sem, page_sem
):
    fetch = fetch_pool(pool_hbm, pool_ref, pool_sem)
    for slot in range(SLOTS):
        meta_vmem[slot : slot + 1] = got_ref[slot, 16:32].astype(jnp.float32)[META_ROW : META_ROW + 1].astype(jnp.int32)
    meta_copy = pltpu.make_async_copy(meta_vmem, meta_ref, meta_sem)
    meta_copy.start()
    ret_ref[...] = jnp.zeros_like(ret_ref)
    meta_copy.wait()
    length_of = lambda slot: meta_ref[slot, 20] * 32 + meta_ref[slot, 21]
    unused = sort_rows(length_of, SLOTS, order_ref)
    unused_ref[0] = unused
    for copy in fetch:
        copy.wait()

    def copies(slot, carry):
        for c in range(COPIED):
            page = meta_ref[slot, PAGES_ROW + c]
            pltpu.make_async_copy(pool_ref.at[:, page], send_ref.at[slot, c], page_sem).start()
        return carry

    lax.fori_loop(0, SLOTS, copies, 0)

    def attend(tokens, slots):
        outputs = attend_group(
            tokens,
            [got_ref[slot, 0:16] for slot in slots],
            [got_ref[slot, 16:32].astype(jnp.float32)[0:8] for slot in slots],
            [[meta_ref[slot, p] for p in range(PAGES_ROW)] for slot in slots],
            [length_of(slot) for slot in slots],
            pool_ref,
            scores_ref,
        )
        for slot, output in zip(slots, outputs):
            ret_ref[slot] = output

    each_group((unused // GROUP, SLOTS // GROUP), order_ref, length_of, attend)
    pltpu.make_async_copy(send_ref, send_ref, page_sem).wait()


def serve(got, after, pool):
    return pl.pallas_call(
        serve_kernel,
        out_shape=(
            jax.ShapeDtypeStruct((SLOTS, 16, HEAD), jnp.bfloat16),
            jax.ShapeDtypeStruct((SLOTS, COPIED, 2, PAGE, HEAD), jnp.bfloat16),
            jax.ShapeDtypeStruct((1,), jnp.int32),
        ),
        in_specs=[VMEM, HBM, HBM],
        out_specs=(VMEM, HBM, SMEM),
        scratch_shapes=attention_scratch(pool)
        + [
            pltpu.VMEM((SLOTS, HEAD), jnp.int32),
            pltpu.SMEM((SLOTS, HEAD), jnp.int32),
            pltpu.SMEM((SLOTS,), jnp.int32),
            pltpu.SemaphoreType.DMA,
            pltpu.SemaphoreType.DMA,
        ],
        compiler_params=PARAMS,
        cost_estimate=pl.CostEstimate(flops=6 * 10**9, bytes_accessed=8 * 2**20, transcendentals=0),
        name="serve_requests",
    )(got, after, pool)


def pick_kernel(slot_ref, got_ref, out_ref, done_ref, held, in_sem, out_sem):
    done_ref[0] = 0.0
    loads = [
        pltpu.make_async_copy(got_ref.at[slot_ref[j]], held.at[j], in_sem.at[j]) for j in range(MIGRANTS)
    ]
    stores = [pltpu.make_async_copy(held.at[j], out_ref.at[j], out_sem.at[j]) for j in range(MIGRANTS)]
    for load in loads:
        load.start()
    for load, store in zip(loads, stores):
        load.wait()
        store.start()
    for store in stores:
        store.wait()


def pick(slots, got):
    shape = (MIGRANTS, COPIED, 2, PAGE, HEAD)
    return pl.pallas_call(
        pick_kernel,
        out_shape=(jax.ShapeDtypeStruct(shape, jnp.bfloat16), jax.ShapeDtypeStruct((1,), jnp.float32)),
        in_specs=[SMEM, HBM],
        out_specs=(HBM, SMEM),
        scratch_shapes=[
            pltpu.VMEM(shape, jnp.bfloat16),
            pltpu.SemaphoreType.DMA((MIGRANTS,)),
            pltpu.SemaphoreType.DMA((MIGRANTS,)),
        ],
        compiler_params=PARAMS,
        name="pick_pages",
    )(slots, got)


def shift_z(value, by):
    pairs = [(z * 2 + x, (z + by) % 4 * 2 + x) for z in range(4) for x in range(2)]
    return lax.ppermute(value, "tensor", pairs)


def swap_x(value):
    return lax.ppermute(value, "tensor", [(t, t ^ 1) for t in range(8)])


def f32_sum(*terms):
    return functools.reduce(jnp.add, [term.astype(jnp.float32) for term in terms])


def reduce_z(own, up, down, up_later, down_later):
    from_below, from_above = shift_z(up, 1), shift_z(down, -1)
    up_later = f32_sum(up_later, from_below[:64]).astype(jnp.bfloat16)
    down_later = f32_sum(down_later, from_above[:64]).astype(jnp.bfloat16)
    first = f32_sum(own[:, :WIDTH], from_above[64:], shift_z(up_later, 1))
    second = f32_sum(own[:, WIDTH:], from_below[64:], shift_z(down_later, -1))
    return jnp.concatenate([first, second], axis=1)


def body(
    queries,
    step_key_value,
    replica_page_store,
    page_table,
    lengths,
    mig_offset,
    copy_order,
    out_weight,
):
    xi = lax.axis_index("tensor") % 2
    pool = replica_page_store[0]
    query = queries[0].reshape(ROWS, 2, 8, HEAD).transpose(0, 2, 1, 3)
    fresh = step_key_value[0]
    table = page_table[0].T
    payload, slots = request(
        mig_offset[:, :, 0], copy_order.transpose(1, 0, 2), table, lengths, query, fresh
    )
    got = lax.all_to_all(
        payload.reshape(REPLICAS, CAP, 32, HEAD), "replica", split_axis=0, concat_axis=0, tiled=True
    ).reshape(SLOTS, 32, HEAD)
    first = stay(table, lengths, query, fresh, pool, FIRST)
    answered, sending, unused = serve(got, first, pool)
    second = attend_second(unused, table, lengths, query, fresh, pool)
    returned = lax.all_to_all(
        answered.reshape(REPLICAS, CAP, 16, HEAD), "replica", split_axis=0, concat_axis=0, tiled=True
    ).reshape(SLOTS, 16, HEAD)
    incoming = lax.all_to_all(
        sending.reshape(REPLICAS, CAP, COPIED, 2, PAGE, HEAD),
        "replica",
        split_axis=0,
        concat_axis=0,
        tiled=True,
    ).reshape(SLOTS, COPIED, 2, PAGE, HEAD)
    merged, zero_parts, one_parts = project(
        slots, table, lengths, query, fresh, pool, first, second, returned, out_weight
    )
    one_parts[1:3] = second_turn(*one_parts[1:3])
    arrived, nothing = pick(slots, incoming)
    finished = []
    for parts in (zero_parts, one_parts):
        total = reduce_z(*parts).reshape(2, 32, 2 * WIDTH)
        mine = lax.dynamic_index_in_dim(total, xi, 0, keepdims=False)
        other = lax.dynamic_index_in_dim(total, 1 - xi, 0, keepdims=False)
        finished.append(mine + swap_x(other.astype(jnp.bfloat16)).astype(jnp.float32))
    finished[1] += nothing[0]
    projected = jnp.concatenate([half.astype(jnp.bfloat16) for half in finished], axis=1).reshape(16, 2, -1)
    attention = merged.transpose(0, 2, 1, 3).reshape(ROWS, 2, 8 * HEAD)
    return (attention[None], projected[None], arrived[None])


def solution(mesh):
    placed = (
        P("replica", None, None, "tensor"),
        P("replica", None, None, None, "tensor"),
        P("replica", None, None, None, "tensor"),
        P("replica", None, None),
        P("replica", None),
        P("replica", None, None),
        P("replica", None, None),
        P("tensor", None),
    )
    return jax.shard_map(
        body,
        mesh=mesh,
        in_specs=placed,
        out_specs=(
            P("replica", None, None, "tensor"),
            P("replica", "tensor", None, None),
            P("replica", None, None, None, None, "tensor"),
        ),
        check_vma=False,
    )
```

```python
import functools
import math

import jax
import jax.numpy as jnp
from jax import lax
from jax.experimental import pallas as pl
from jax.experimental.pallas import tpu as pltpu
from jax.sharding import PartitionSpec as P

HEAD = 128
ROWS = 128
MIGRANTS = 14
STAYING = ROWS - MIGRANTS
COPIED = 4
PAGES_ROW = 16
PAGE = 64
REPLICAS = 16
CAP = 2
SLOTS = REPLICAS * CAP
GROUP = 8
CONTEXT = PAGES_ROW * PAGE
NEG_FILL = -1e30
SCALE = math.log2(math.e) / math.sqrt(HEAD)
META_ROW = 4
CHUNK = 256
FIRST = 48
SECOND = 32
THIRD = 40
WIDTH = 2048
WEIGHT_TILE = 1024
WEIGHT_PARTS = 8
VMEM = pl.BlockSpec(memory_space=pltpu.VMEM)
SMEM = pl.BlockSpec(memory_space=pltpu.SMEM)
HBM = pl.BlockSpec(memory_space=pltpu.HBM)
PARAMS = pltpu.CompilerParams(vmem_limit_bytes=60 * 2**20)
ROOMY = pltpu.CompilerParams(vmem_limit_bytes=52 * 2**20)


def attend_group(tokens, queries, fresh, pages, lengths, pool_ref, scores_ref):
    nt = (((1,), (1,)), ((), ()))
    for i in range(GROUP):
        keys = jnp.concatenate([pool_ref[0, page] for page in pages[i][: tokens // PAGE]], axis=0)
        scores_ref[i, :, 0:tokens] = lax.dot_general(
            queries[i], keys, nt, preferred_element_type=jnp.float32
        )
        scores_ref[i, :, CONTEXT : CONTEXT + 8] = lax.dot_general(
            queries[i], fresh[i].astype(jnp.bfloat16), nt, preferred_element_type=jnp.float32
        )
    outputs = []
    for i in range(GROUP):
        scores = scores_ref[i, :, 0:tokens]
        position = lax.broadcasted_iota(jnp.int32, scores.shape, 1)
        scores = jnp.where(position < lengths[i], scores, NEG_FILL)
        fresh_scores = scores_ref[i, :, CONTEXT : CONTEXT + 8]
        line = lax.broadcasted_iota(jnp.int32, fresh_scores.shape, 1)
        step = lax.rem(lax.broadcasted_iota(jnp.int32, fresh_scores.shape, 0), 2)
        fresh_scores = jnp.where((line == 0) | (line == 2 * step), fresh_scores, NEG_FILL)
        highest = jnp.maximum(
            jnp.max(scores, axis=1, keepdims=True), jnp.max(fresh_scores, axis=1, keepdims=True)
        )
        weights = jnp.exp2((scores - highest) * SCALE).astype(jnp.bfloat16)
        fresh_weights = jnp.exp2((fresh_scores - highest) * SCALE).astype(jnp.bfloat16)
        total = jnp.sum(weights.astype(jnp.float32), axis=1, keepdims=True) + jnp.sum(
            fresh_weights.astype(jnp.float32), axis=1, keepdims=True
        )
        values = jnp.concatenate([pool_ref[1, page] for page in pages[i][: tokens // PAGE]], axis=0)
        fresh_values = pltpu.roll(fresh[i], 7, 0).astype(jnp.bfloat16)
        weighted = jnp.dot(weights, values, preferred_element_type=jnp.float32) + jnp.dot(
            fresh_weights, fresh_values, preferred_element_type=jnp.float32
        )
        outputs.append((weighted / total).astype(jnp.bfloat16))
    return outputs


def fresh_rows(tokens):
    tokens = tokens.astype(jnp.float32).reshape(4, HEAD)
    return jnp.concatenate([tokens, jnp.zeros((4, HEAD), jnp.float32)], axis=0)


def fetch_pool(pool_hbm, pool_ref, sem):
    copies = [
        pltpu.make_async_copy(pool_hbm.at[k, p : p + 32], pool_ref.at[k, p : p + 32], sem.at[k, p // 32])
        for k in range(2)
        for p in range(0, 128, 32)
    ]
    for copy in copies:
        copy.start()
    return copies


def chunks_of(length):
    return (length + CHUNK - 1) // CHUNK


def sort_rows(length_of, count, order_ref):
    def tally(i, counts):
        chunks = chunks_of(length_of(i))
        return tuple(c + jnp.where(chunks == k, 1, 0) for k, c in enumerate(counts))

    zero = jnp.int32(0)
    counts = lax.fori_loop(0, count, tally, (zero,) * 5)
    starts = [zero]
    for c in counts[:4]:
        starts.append(starts[-1] + c)

    def put(i, starts):
        chunks = chunks_of(length_of(i))
        place = zero
        for k in range(5):
            place = jnp.where(chunks == k, starts[k], place)
        order_ref[place] = i
        return tuple(s + jnp.where(chunks == k, 1, 0) for k, s in enumerate(starts))

    lax.fori_loop(0, count, put, tuple(starts))
    return counts[0]


def each_group(groups, order_ref, length_of, attend):
    def group(g, carry):
        rows = [order_ref[g * GROUP + i] for i in range(GROUP)]
        chunks = jnp.maximum(chunks_of(length_of(rows[-1])), 1)
        for k in range(1, CONTEXT // CHUNK + 1):

            @pl.when(chunks == k)
            def _():
                attend(k * CHUNK, rows)

        return carry

    lax.fori_loop(groups[0], groups[1], group, 0)


def stay_copies(first, count, query_hbm, fresh_hbm, query_ref, fresh_ref, sem):
    copies = [
        pltpu.make_async_copy(query_hbm.at[first : first + count], query_ref, sem.at[0]),
        pltpu.make_async_copy(fresh_hbm.at[first : first + count], fresh_ref, sem.at[1]),
    ]
    for copy in copies:
        copy.start()
    return copies


def attend_staying(
    first, count, table_ref, length_ref, query_hbm, fresh_hbm, pool_hbm, out_ref, out_first, refs, meanwhile=None
):
    pool_ref, scores_ref, pool_sem, query_ref, fresh_ref, order_ref, row_sem = refs
    copies = fetch_pool(pool_hbm, pool_ref, pool_sem)
    copies += stay_copies(first, count, query_hbm, fresh_hbm, query_ref, fresh_ref, row_sem)
    length_of = lambda i: jnp.where(first + i < STAYING, length_ref[0, first + i], 1)
    sort_rows(length_of, count, order_ref)
    for copy in copies:
        copy.wait()
    started = meanwhile() if meanwhile is not None else None

    def attend(tokens, rows):
        outputs = attend_group(
            tokens,
            [query_ref[row].reshape(16, HEAD) for row in rows],
            [fresh_rows(fresh_ref[row]) for row in rows],
            [[table_ref[p, first + row] for p in range(PAGES_ROW)] for row in rows],
            [length_of(row) for row in rows],
            pool_ref,
            scores_ref,
        )
        for row, output in zip(rows, outputs):
            out_ref[out_first + row] = output.reshape(8, 2, HEAD)

    each_group((0, count // GROUP), order_ref, length_of, attend)
    return started


def stay_kernel(table_ref, length_ref, query_hbm, fresh_hbm, pool_hbm, out_ref, turn_ref, *refs):
    turn_ref[...] = jnp.zeros_like(turn_ref)
    attend_staying(0, FIRST, table_ref, length_ref, query_hbm, fresh_hbm, pool_hbm, out_ref, 0, refs)


def attention_scratch(pool):
    return [
        pltpu.VMEM(pool.shape, pool.dtype),
        pltpu.VMEM((GROUP, 16, CONTEXT + 128), jnp.float32),
        pltpu.SemaphoreType.DMA((2, 4)),
    ]


def stay_scratch(pool, count):
    return attention_scratch(pool) + [
        pltpu.VMEM((count, 8, 2, HEAD), jnp.bfloat16),
        pltpu.VMEM((count, 2, 2, HEAD), jnp.bfloat16),
        pltpu.SMEM((count,), jnp.int32),
        pltpu.SemaphoreType.DMA((2,)),
    ]


def stay(table, lengths, query, fresh, pool, count):
    return pl.pallas_call(
        stay_kernel,
        out_shape=(jax.ShapeDtypeStruct((count, 8, 2, HEAD), jnp.bfloat16), pltpu.VMEM((8, HEAD), jnp.float32)),
        in_specs=[SMEM, SMEM, HBM, HBM, HBM],
        out_specs=(VMEM, VMEM),
        scratch_shapes=stay_scratch(pool, count),
        compiler_params=PARAMS,
        cost_estimate=pl.CostEstimate(flops=8 * 10**9, bytes_accessed=8 * 2**20, transcendentals=0),
        name="attend_first",
    )(table, lengths, query, fresh, pool)


def fetch_weight(weight_hbm, weight_ref, sem):
    copies = []
    for c in range(WEIGHT_PARTS):
        columns = slice(c * WEIGHT_TILE, (c + 1) * WEIGHT_TILE)
        copies.append(pltpu.make_async_copy(weight_hbm.at[:, columns], weight_ref.at[:, columns], sem.at[c]))
    for copy in copies:
        copy.start()
    return copies


def second_kernel(after_ref, table_ref, length_ref, query_hbm, fresh_hbm, pool_hbm, out_ref, *refs):
    attend_staying(FIRST, SECOND, table_ref, length_ref, query_hbm, fresh_hbm, pool_hbm, out_ref, 0, refs)


def attend_second(after, table, lengths, query, fresh, pool):
    return pl.pallas_call(
        second_kernel,
        out_shape=jax.ShapeDtypeStruct((SECOND, 8, 2, HEAD), jnp.bfloat16),
        in_specs=[SMEM, SMEM, SMEM, HBM, HBM, HBM],
        out_specs=VMEM,
        scratch_shapes=stay_scratch(pool, SECOND),
        compiler_params=PARAMS,
        cost_estimate=pl.CostEstimate(flops=8 * 10**9, bytes_accessed=8 * 2**20, transcendentals=0),
        name="attend_second",
    )(after, table, lengths, query, fresh, pool)


def project_rolled(rolled_ref, weight_ref, fetch, held_refs, part_refs, sem):
    copies = []
    for c, copy in enumerate(fetch):
        copy.wait()
        start = c * WEIGHT_TILE
        product = jnp.dot(
            rolled_ref[...], weight_ref[:, start : start + WEIGHT_TILE], preferred_element_type=jnp.float32
        ).astype(jnp.bfloat16)
        half, start = divmod(start, 2 * WIDTH)
        own, above, far, below = (product[64 * k : 64 * k + 64] for k in range(4))
        place = slice(start % WIDTH, start % WIDTH + WEIGHT_TILE)
        first, second = slice(0, 64), slice(64, 128)
        if start < WIDTH:
            puts = [(1, first, far), (2, second, below), (3, first, above)]
        else:
            puts = [(2, first, far), (1, second, above), (4, first, below)]
        puts = [(part, lines, place, value) for part, lines, value in puts]
        puts.append((0, first, slice(start, start + WEIGHT_TILE), own))
        for k, (part, lines, columns, value) in enumerate(puts):
            held, target = held_refs[half * 5 + part], part_refs[half * 5 + part]
            held[lines, columns] = value
            copies.append(pltpu.make_async_copy(held.at[lines, columns], target.at[lines, columns], sem.at[c, k]))
            copies[-1].start()
    return copies


PART_SHAPES = ((64, 2 * WIDTH), (128, WIDTH), (128, WIDTH), (64, WIDTH), (64, WIDTH)) * 2


def project_kernel(
    slot_ref, table_ref, length_ref, query_hbm, fresh_hbm, pool_hbm, first_ref, second_ref, ret_ref, weight_hbm,
    out_ref, *refs
):
    part_refs, refs = refs[:10], refs[10:]
    stay_refs, held_refs, (weight_ref, rolled_ref, weight_sem, part_sem) = refs[:-14], refs[-14:-4], refs[-4:]
    done = FIRST + SECOND

    def start_weight():
        return fetch_weight(weight_hbm, weight_ref, weight_sem)

    fetch = attend_staying(
        done, THIRD, table_ref, length_ref, query_hbm, fresh_hbm, pool_hbm, out_ref, done, stay_refs, start_weight
    )
    out_ref[0:FIRST] = first_ref[...]
    out_ref[FIRST:done] = second_ref[...]
    for j in range(MIGRANTS):
        out_ref[STAYING + j] = ret_ref[slot_ref[j]].reshape(8, 2, HEAD)
    zi = lax.axis_index("tensor") // 2
    for z in range(4):
        place = pl.multiple_of(lax.rem(z - zi + 4, 4) * 64, 64)
        for h in range(8):
            rolled_ref[pl.ds(place, 64), h * HEAD : (h + 1) * HEAD] = out_ref[32 * z : 32 * z + 32, h].reshape(64, HEAD)
    for copy in project_rolled(rolled_ref, weight_ref, fetch, held_refs, part_refs, part_sem):
        copy.wait()


def project(slots, table, lengths, query, fresh, pool, first, second, returned, weight):
    out = pl.pallas_call(
        project_kernel,
        out_shape=[jax.ShapeDtypeStruct((ROWS, 8, 2, HEAD), jnp.bfloat16)]
        + [jax.ShapeDtypeStruct(shape, jnp.bfloat16) for shape in PART_SHAPES],
        in_specs=[SMEM, SMEM, SMEM, HBM, HBM, HBM, VMEM, VMEM, VMEM, HBM],
        out_specs=[VMEM] + [HBM] * 10,
        scratch_shapes=stay_scratch(pool, THIRD)
        + [pltpu.VMEM(shape, jnp.bfloat16) for shape in PART_SHAPES]
        + [
            pltpu.VMEM(weight.shape, weight.dtype),
            pltpu.VMEM((2 * ROWS, weight.shape[0]), jnp.bfloat16),
            pltpu.SemaphoreType.DMA((WEIGHT_PARTS,)),
            pltpu.SemaphoreType.DMA((WEIGHT_PARTS, 4)),
        ],
        compiler_params=ROOMY,
        cost_estimate=pl.CostEstimate(flops=10**9, bytes_accessed=2**20, transcendentals=0),
        name="attend_third_project",
    )(slots, table, lengths, query, fresh, pool, first, second, returned, weight)
    return out[0], list(out[1:6]), list(out[6:])


def same_kernel(*refs):
    pass


def second_turn(up, down):
    return pl.pallas_call(
        same_kernel,
        out_shape=[jax.ShapeDtypeStruct(x.shape, x.dtype) for x in (up, down)],
        in_specs=[HBM, HBM],
        out_specs=[HBM, HBM],
        input_output_aliases={0: 0, 1: 1},
        compiler_params=PARAMS,
        cost_estimate=pl.CostEstimate(flops=3 * 10**10, bytes_accessed=2**20, transcendentals=0),
        name="second_turn",
    )(up, down)


def request_kernel(
    offset_ref, order_ref, table_ref, length_ref, query_ref, fresh_ref, out_ref, slot_ref, used
):
    own = lax.axis_index("replica")
    out_ref[...] = jnp.zeros_like(out_ref)
    for s in range(REPLICAS):
        used[s] = 0
    lane = lax.broadcasted_iota(jnp.int32, (1, HEAD), 1)
    for j in range(MIGRANTS):
        row = STAYING + j
        source = lax.rem(own + 1 + offset_ref[0, j], REPLICAS)
        rank = used[source]
        used[source] = rank + 1
        slot = source * CAP + rank
        slot_ref[j] = slot
        meta = jnp.zeros((1, HEAD), jnp.int32)
        for p in range(PAGES_ROW):
            meta = jnp.where(lane == p, table_ref[p, row], meta)
        for c in range(COPIED):
            wanted = table_ref[order_ref[j, 0, c], row]
            meta = jnp.where(lane == PAGES_ROW + c, wanted, meta)
        length = length_ref[0, row]
        meta = jnp.where(lane == 20, length // 32, meta)
        meta = jnp.where(lane == 21, lax.rem(length, 32), meta)
        out_ref[slot, 0:16] = query_ref[row - (ROWS - 16)].reshape(16, HEAD)
        out_ref[slot, 16:32] = jnp.concatenate(
            [
                fresh_ref[row - (ROWS - 16)].astype(jnp.float32).reshape(4, HEAD),
                meta.astype(jnp.float32),
                jnp.zeros((11, HEAD), jnp.float32),
            ],
            axis=0,
        ).astype(jnp.bfloat16)


def request(offsets, order, table, lengths, query, fresh):
    return pl.pallas_call(
        request_kernel,
        out_shape=(
            jax.ShapeDtypeStruct((SLOTS, 32, HEAD), jnp.bfloat16),
            jax.ShapeDtypeStruct((MIGRANTS,), jnp.int32),
        ),
        grid=(1,),
        in_specs=[SMEM] * 4
        + [pl.BlockSpec((16, 8, 2, HEAD), lambda i: (7, 0, 0, 0)), pl.BlockSpec((16, 2, 2, HEAD), lambda i: (7, 0, 0, 0))],
        out_specs=(VMEM, SMEM),
        scratch_shapes=[pltpu.SMEM((REPLICAS,), jnp.int32)],
        compiler_params=PARAMS,
        name="pack_requests",
    )(offsets, order, table, lengths, query, fresh)


def serve_kernel(
    got_ref, after_ref, pool_hbm, ret_ref, send_ref, unused_ref, pool_ref, scores_ref, pool_sem, meta_vmem, meta_ref, order_ref,
    meta_sem, page_sem
):
    fetch = fetch_pool(pool_hbm, pool_ref, pool_sem)
    for slot in range(SLOTS):
        meta_vmem[slot : slot + 1] = got_ref[slot, 16:32].astype(jnp.float32)[META_ROW : META_ROW + 1].astype(jnp.int32)
    meta_copy = pltpu.make_async_copy(meta_vmem, meta_ref, meta_sem)
    meta_copy.start()
    ret_ref[...] = jnp.zeros_like(ret_ref)
    meta_copy.wait()
    length_of = lambda slot: meta_ref[slot, 20] * 32 + meta_ref[slot, 21]
    unused = sort_rows(length_of, SLOTS, order_ref)
    unused_ref[0] = unused
    for copy in fetch:
        copy.wait()

    def copies(slot, carry):
        for c in range(COPIED):
            page = meta_ref[slot, PAGES_ROW + c]
            pltpu.make_async_copy(pool_ref.at[:, page], send_ref.at[slot, c], page_sem).start()
        return carry

    lax.fori_loop(0, SLOTS, copies, 0)

    def attend(tokens, slots):
        outputs = attend_group(
            tokens,
            [got_ref[slot, 0:16] for slot in slots],
            [got_ref[slot, 16:32].astype(jnp.float32)[0:8] for slot in slots],
            [[meta_ref[slot, p] for p in range(PAGES_ROW)] for slot in slots],
            [length_of(slot) for slot in slots],
            pool_ref,
            scores_ref,
        )
        for slot, output in zip(slots, outputs):
            ret_ref[slot] = output

    each_group((unused // GROUP, SLOTS // GROUP), order_ref, length_of, attend)
    pltpu.make_async_copy(send_ref, send_ref, page_sem).wait()


def serve(got, after, pool):
    return pl.pallas_call(
        serve_kernel,
        out_shape=(
            jax.ShapeDtypeStruct((SLOTS, 16, HEAD), jnp.bfloat16),
            jax.ShapeDtypeStruct((SLOTS, COPIED, 2, PAGE, HEAD), jnp.bfloat16),
            jax.ShapeDtypeStruct((1,), jnp.int32),
        ),
        in_specs=[VMEM, VMEM, HBM],
        out_specs=(VMEM, HBM, SMEM),
        scratch_shapes=attention_scratch(pool)
        + [
            pltpu.VMEM((SLOTS, HEAD), jnp.int32),
            pltpu.SMEM((SLOTS, HEAD), jnp.int32),
            pltpu.SMEM((SLOTS,), jnp.int32),
            pltpu.SemaphoreType.DMA,
            pltpu.SemaphoreType.DMA,
        ],
        compiler_params=ROOMY,
        cost_estimate=pl.CostEstimate(flops=6 * 10**9, bytes_accessed=8 * 2**20, transcendentals=0),
        name="serve_requests",
    )(got, after, pool)


def pick_kernel(slot_ref, got_ref, out_ref, done_ref, held, in_sem, out_sem):
    done_ref[0] = 0.0
    loads = [
        pltpu.make_async_copy(got_ref.at[slot_ref[j]], held.at[j], in_sem.at[j]) for j in range(MIGRANTS)
    ]
    stores = [pltpu.make_async_copy(held.at[j], out_ref.at[j], out_sem.at[j]) for j in range(MIGRANTS)]
    for load in loads:
        load.start()
    for load, store in zip(loads, stores):
        load.wait()
        store.start()
    for store in stores:
        store.wait()


def pick(slots, got):
    shape = (MIGRANTS, COPIED, 2, PAGE, HEAD)
    return pl.pallas_call(
        pick_kernel,
        out_shape=(jax.ShapeDtypeStruct(shape, jnp.bfloat16), jax.ShapeDtypeStruct((1,), jnp.float32)),
        in_specs=[SMEM, HBM],
        out_specs=(HBM, SMEM),
        scratch_shapes=[
            pltpu.VMEM(shape, jnp.bfloat16),
            pltpu.SemaphoreType.DMA((MIGRANTS,)),
            pltpu.SemaphoreType.DMA((MIGRANTS,)),
        ],
        compiler_params=PARAMS,
        name="pick_pages",
    )(slots, got)


def shift_z(value, by):
    pairs = [(z * 2 + x, (z + by) % 4 * 2 + x) for z in range(4) for x in range(2)]
    return lax.ppermute(value, "tensor", pairs)


def swap_x(value):
    return lax.ppermute(value, "tensor", [(t, t ^ 1) for t in range(8)])


def f32_sum(*terms):
    return functools.reduce(jnp.add, [term.astype(jnp.float32) for term in terms])


def reduce_z(own, up, down, up_later, down_later):
    from_below, from_above = shift_z(up, 1), shift_z(down, -1)
    up_later = f32_sum(up_later, from_below[:64]).astype(jnp.bfloat16)
    down_later = f32_sum(down_later, from_above[:64]).astype(jnp.bfloat16)
    first = f32_sum(own[:, :WIDTH], from_above[64:], shift_z(up_later, 1))
    second = f32_sum(own[:, WIDTH:], from_below[64:], shift_z(down_later, -1))
    return jnp.concatenate([first, second], axis=1)


def body(
    queries,
    step_key_value,
    replica_page_store,
    page_table,
    lengths,
    mig_offset,
    copy_order,
    out_weight,
):
    xi = lax.axis_index("tensor") % 2
    pool = replica_page_store[0]
    query = queries[0].reshape(ROWS, 2, 8, HEAD).transpose(0, 2, 1, 3)
    fresh = step_key_value[0]
    table = page_table[0].T
    payload, slots = request(
        mig_offset[:, :, 0], copy_order.transpose(1, 0, 2), table, lengths, query, fresh
    )
    got = lax.all_to_all(
        payload.reshape(REPLICAS, CAP, 32, HEAD), "replica", split_axis=0, concat_axis=0, tiled=True
    ).reshape(SLOTS, 32, HEAD)
    first, turn = stay(table, lengths, query, fresh, pool, FIRST)
    answered, sending, unused = serve(got, turn, pool)
    second = attend_second(unused, table, lengths, query, fresh, pool)
    returned = lax.all_to_all(
        answered.reshape(REPLICAS, CAP, 16, HEAD), "replica", split_axis=0, concat_axis=0, tiled=True
    ).reshape(SLOTS, 16, HEAD)
    incoming = lax.all_to_all(
        sending.reshape(REPLICAS, CAP, COPIED, 2, PAGE, HEAD),
        "replica",
        split_axis=0,
        concat_axis=0,
        tiled=True,
    ).reshape(SLOTS, COPIED, 2, PAGE, HEAD)
    merged, zero_parts, one_parts = project(
        slots, table, lengths, query, fresh, pool, first, second, returned, out_weight
    )
    one_parts[1:3] = second_turn(*one_parts[1:3])
    arrived, nothing = pick(slots, incoming)
    finished = []
    for parts in (zero_parts, one_parts):
        total = reduce_z(*parts).reshape(2, 32, 2 * WIDTH)
        mine = lax.dynamic_index_in_dim(total, xi, 0, keepdims=False)
        other = lax.dynamic_index_in_dim(total, 1 - xi, 0, keepdims=False)
        finished.append(mine + swap_x(other.astype(jnp.bfloat16)).astype(jnp.float32))
    finished[1] += nothing[0]
    projected = jnp.concatenate([half.astype(jnp.bfloat16) for half in finished], axis=1).reshape(16, 2, -1)
    attention = merged.transpose(0, 2, 1, 3).reshape(ROWS, 2, 8 * HEAD)
    return (attention[None], projected[None], arrived[None])


def solution(mesh):
    placed = (
        P("replica", None, None, "tensor"),
        P("replica", None, None, None, "tensor"),
        P("replica", None, None, None, "tensor"),
        P("replica", None, None),
        P("replica", None),
        P("replica", None, None),
        P("replica", None, None),
        P("tensor", None),
    )
    return jax.shard_map(
        body,
        mesh=mesh,
        in_specs=placed,
        out_specs=(
            P("replica", None, None, "tensor"),
            P("replica", "tensor", None, None),
            P("replica", None, None, None, None, "tensor"),
        ),
        check_vma=False,
    )
```

```python
import functools
import math

import jax
import jax.numpy as jnp
from jax import lax
from jax.experimental import pallas as pl
from jax.experimental.pallas import tpu as pltpu
from jax.sharding import PartitionSpec as P

HEAD = 128
ROWS = 128
MIGRANTS = 14
STAYING = ROWS - MIGRANTS
COPIED = 4
PAGES_ROW = 16
PAGE = 64
REPLICAS = 16
CAP = 2
SLOTS = REPLICAS * CAP
GROUP = 8
CONTEXT = PAGES_ROW * PAGE
NEG_FILL = -1e30
SCALE = math.log2(math.e) / math.sqrt(HEAD)
META_ROW = 4
CHUNK = 256
FIRST = 40
SECOND = 32
THIRD = 48
WIDTH = 2048
WEIGHT_TILE = 1024
WEIGHT_PARTS = 8
VMEM = pl.BlockSpec(memory_space=pltpu.VMEM)
SMEM = pl.BlockSpec(memory_space=pltpu.SMEM)
HBM = pl.BlockSpec(memory_space=pltpu.HBM)
PARAMS = pltpu.CompilerParams(vmem_limit_bytes=60 * 2**20)
ROOMY = pltpu.CompilerParams(vmem_limit_bytes=52 * 2**20)


def attend_group(tokens, queries, fresh, pages, lengths, pool_ref, scores_ref):
    nt = (((1,), (1,)), ((), ()))
    for i in range(GROUP):
        keys = jnp.concatenate([pool_ref[0, page] for page in pages[i][: tokens // PAGE]], axis=0)
        scores_ref[i, :, 0:tokens] = lax.dot_general(
            queries[i], keys, nt, preferred_element_type=jnp.float32
        )
        scores_ref[i, :, CONTEXT : CONTEXT + 8] = lax.dot_general(
            queries[i], fresh[i].astype(jnp.bfloat16), nt, preferred_element_type=jnp.float32
        )
    outputs = []
    for i in range(GROUP):
        scores = scores_ref[i, :, 0:tokens]
        position = lax.broadcasted_iota(jnp.int32, scores.shape, 1)
        scores = jnp.where(position < lengths[i], scores, NEG_FILL)
        fresh_scores = scores_ref[i, :, CONTEXT : CONTEXT + 8]
        line = lax.broadcasted_iota(jnp.int32, fresh_scores.shape, 1)
        step = lax.rem(lax.broadcasted_iota(jnp.int32, fresh_scores.shape, 0), 2)
        fresh_scores = jnp.where((line == 0) | (line == 2 * step), fresh_scores, NEG_FILL)
        highest = jnp.maximum(
            jnp.max(scores, axis=1, keepdims=True), jnp.max(fresh_scores, axis=1, keepdims=True)
        )
        weights = jnp.exp2((scores - highest) * SCALE).astype(jnp.bfloat16)
        fresh_weights = jnp.exp2((fresh_scores - highest) * SCALE).astype(jnp.bfloat16)
        total = jnp.sum(weights.astype(jnp.float32), axis=1, keepdims=True) + jnp.sum(
            fresh_weights.astype(jnp.float32), axis=1, keepdims=True
        )
        values = jnp.concatenate([pool_ref[1, page] for page in pages[i][: tokens // PAGE]], axis=0)
        fresh_values = pltpu.roll(fresh[i], 7, 0).astype(jnp.bfloat16)
        weighted = jnp.dot(weights, values, preferred_element_type=jnp.float32) + jnp.dot(
            fresh_weights, fresh_values, preferred_element_type=jnp.float32
        )
        outputs.append((weighted / total).astype(jnp.bfloat16))
    return outputs


def fresh_rows(tokens):
    tokens = tokens.astype(jnp.float32).reshape(4, HEAD)
    return jnp.concatenate([tokens, jnp.zeros((4, HEAD), jnp.float32)], axis=0)


def fetch_pool(pool_hbm, pool_ref, sem):
    copies = [
        pltpu.make_async_copy(pool_hbm.at[k, p : p + 32], pool_ref.at[k, p : p + 32], sem.at[k, p // 32])
        for k in range(2)
        for p in range(0, 128, 32)
    ]
    for copy in copies:
        copy.start()
    return copies


def chunks_of(length):
    return (length + CHUNK - 1) // CHUNK


def sort_rows(length_of, count, order_ref):
    def tally(i, counts):
        chunks = chunks_of(length_of(i))
        return tuple(c + jnp.where(chunks == k, 1, 0) for k, c in enumerate(counts))

    zero = jnp.int32(0)
    counts = lax.fori_loop(0, count, tally, (zero,) * 5)
    starts = [zero]
    for c in counts[:4]:
        starts.append(starts[-1] + c)

    def put(i, starts):
        chunks = chunks_of(length_of(i))
        place = zero
        for k in range(5):
            place = jnp.where(chunks == k, starts[k], place)
        order_ref[place] = i
        return tuple(s + jnp.where(chunks == k, 1, 0) for k, s in enumerate(starts))

    lax.fori_loop(0, count, put, tuple(starts))
    return counts[0]


def each_group(groups, order_ref, length_of, attend):
    def group(g, carry):
        rows = [order_ref[g * GROUP + i] for i in range(GROUP)]
        chunks = jnp.maximum(chunks_of(length_of(rows[-1])), 1)
        for k in range(1, CONTEXT // CHUNK + 1):

            @pl.when(chunks == k)
            def _():
                attend(k * CHUNK, rows)

        return carry

    lax.fori_loop(groups[0], groups[1], group, 0)


def stay_copies(first, count, query_hbm, fresh_hbm, query_ref, fresh_ref, sem):
    copies = [
        pltpu.make_async_copy(query_hbm.at[first : first + count], query_ref, sem.at[0]),
        pltpu.make_async_copy(fresh_hbm.at[first : first + count], fresh_ref, sem.at[1]),
    ]
    for copy in copies:
        copy.start()
    return copies


def attend_staying(
    first, count, table_ref, length_ref, query_hbm, fresh_hbm, pool_hbm, out_ref, out_first, refs, meanwhile=None
):
    pool_ref, scores_ref, pool_sem, query_ref, fresh_ref, order_ref, row_sem = refs
    copies = fetch_pool(pool_hbm, pool_ref, pool_sem)
    copies += stay_copies(first, count, query_hbm, fresh_hbm, query_ref, fresh_ref, row_sem)
    length_of = lambda i: jnp.where(first + i < STAYING, length_ref[0, first + i], 1)
    sort_rows(length_of, count, order_ref)
    for copy in copies:
        copy.wait()
    started = meanwhile() if meanwhile is not None else None

    def attend(tokens, rows):
        outputs = attend_group(
            tokens,
            [query_ref[row].reshape(16, HEAD) for row in rows],
            [fresh_rows(fresh_ref[row]) for row in rows],
            [[table_ref[p, first + row] for p in range(PAGES_ROW)] for row in rows],
            [length_of(row) for row in rows],
            pool_ref,
            scores_ref,
        )
        for row, output in zip(rows, outputs):
            out_ref[out_first + row] = output.reshape(8, 2, HEAD)

    each_group((0, count // GROUP), order_ref, length_of, attend)
    return started


def stay_kernel(table_ref, length_ref, query_hbm, fresh_hbm, pool_hbm, out_ref, turn_ref, *refs):
    turn_ref[...] = jnp.zeros_like(turn_ref)
    attend_staying(0, FIRST, table_ref, length_ref, query_hbm, fresh_hbm, pool_hbm, out_ref, 0, refs)


def attention_scratch(pool):
    return [
        pltpu.VMEM(pool.shape, pool.dtype),
        pltpu.VMEM((GROUP, 16, CONTEXT + 128), jnp.float32),
        pltpu.SemaphoreType.DMA((2, 4)),
    ]


def stay_scratch(pool, count):
    return attention_scratch(pool) + [
        pltpu.VMEM((count, 8, 2, HEAD), jnp.bfloat16),
        pltpu.VMEM((count, 2, 2, HEAD), jnp.bfloat16),
        pltpu.SMEM((count,), jnp.int32),
        pltpu.SemaphoreType.DMA((2,)),
    ]


def stay(table, lengths, query, fresh, pool, count):
    return pl.pallas_call(
        stay_kernel,
        out_shape=(jax.ShapeDtypeStruct((count, 8, 2, HEAD), jnp.bfloat16), pltpu.VMEM((8, HEAD), jnp.float32)),
        in_specs=[SMEM, SMEM, HBM, HBM, HBM],
        out_specs=(VMEM, VMEM),
        scratch_shapes=stay_scratch(pool, count),
        compiler_params=PARAMS,
        cost_estimate=pl.CostEstimate(flops=8 * 10**9, bytes_accessed=8 * 2**20, transcendentals=0),
        name="attend_first",
    )(table, lengths, query, fresh, pool)


def fetch_weight(weight_hbm, weight_ref, sem):
    copies = []
    for c in range(WEIGHT_PARTS):
        columns = slice(c * WEIGHT_TILE, (c + 1) * WEIGHT_TILE)
        copies.append(pltpu.make_async_copy(weight_hbm.at[:, columns], weight_ref.at[:, columns], sem.at[c]))
    for copy in copies:
        copy.start()
    return copies


def second_kernel(after_ref, table_ref, length_ref, query_hbm, fresh_hbm, pool_hbm, out_ref, *refs):
    attend_staying(FIRST, SECOND, table_ref, length_ref, query_hbm, fresh_hbm, pool_hbm, out_ref, 0, refs)


def attend_second(after, table, lengths, query, fresh, pool):
    return pl.pallas_call(
        second_kernel,
        out_shape=jax.ShapeDtypeStruct((SECOND, 8, 2, HEAD), jnp.bfloat16),
        in_specs=[SMEM, SMEM, SMEM, HBM, HBM, HBM],
        out_specs=VMEM,
        scratch_shapes=stay_scratch(pool, SECOND),
        compiler_params=ROOMY,
        cost_estimate=pl.CostEstimate(flops=8 * 10**9, bytes_accessed=8 * 2**20, transcendentals=0),
        name="attend_second",
    )(after, table, lengths, query, fresh, pool)


def project_rolled(rolled_ref, weight_ref, fetch, held_refs, part_refs, sem):
    copies = []
    for c, copy in enumerate(fetch):
        copy.wait()
        start = c * WEIGHT_TILE
        product = jnp.dot(
            rolled_ref[...], weight_ref[:, start : start + WEIGHT_TILE], preferred_element_type=jnp.float32
        ).astype(jnp.bfloat16)
        half, start = divmod(start, 2 * WIDTH)
        own, above, far, below = (product[64 * k : 64 * k + 64] for k in range(4))
        place = slice(start % WIDTH, start % WIDTH + WEIGHT_TILE)
        first, second = slice(0, 64), slice(64, 128)
        if start < WIDTH:
            puts = [(1, first, far), (2, second, below), (3, first, above)]
        else:
            puts = [(2, first, far), (1, second, above), (4, first, below)]
        puts = [(part, lines, place, value) for part, lines, value in puts]
        puts.append((0, first, slice(start, start + WEIGHT_TILE), own))
        for k, (part, lines, columns, value) in enumerate(puts):
            held, target = held_refs[half * 5 + part], part_refs[half * 5 + part]
            held[lines, columns] = value
            copies.append(pltpu.make_async_copy(held.at[lines, columns], target.at[lines, columns], sem.at[c, k]))
            copies[-1].start()
    return copies


PART_SHAPES = ((64, 2 * WIDTH), (128, WIDTH), (128, WIDTH), (64, WIDTH), (64, WIDTH)) * 2


def project_kernel(
    slot_ref, table_ref, length_ref, query_hbm, fresh_hbm, pool_hbm, first_ref, second_ref, ret_ref, weight_hbm,
    out_ref, *refs
):
    part_refs, refs = refs[:10], refs[10:]
    stay_refs, held_refs, (weight_ref, rolled_ref, weight_sem, part_sem) = refs[:-14], refs[-14:-4], refs[-4:]
    done = FIRST + SECOND

    def start_weight():
        return fetch_weight(weight_hbm, weight_ref, weight_sem)

    fetch = attend_staying(
        done, THIRD, table_ref, length_ref, query_hbm, fresh_hbm, pool_hbm, out_ref, done, stay_refs, start_weight
    )
    out_ref[0:FIRST] = first_ref[...]
    out_ref[FIRST:done] = second_ref[...]
    for j in range(MIGRANTS):
        out_ref[STAYING + j] = ret_ref[slot_ref[j]].reshape(8, 2, HEAD)
    zi = lax.axis_index("tensor") // 2
    for z in range(4):
        place = pl.multiple_of(lax.rem(z - zi + 4, 4) * 64, 64)
        for h in range(8):
            rolled_ref[pl.ds(place, 64), h * HEAD : (h + 1) * HEAD] = out_ref[32 * z : 32 * z + 32, h].reshape(64, HEAD)
    for copy in project_rolled(rolled_ref, weight_ref, fetch, held_refs, part_refs, part_sem):
        copy.wait()


def project(slots, table, lengths, query, fresh, pool, first, second, returned, weight):
    out = pl.pallas_call(
        project_kernel,
        out_shape=[jax.ShapeDtypeStruct((ROWS, 8, 2, HEAD), jnp.bfloat16)]
        + [jax.ShapeDtypeStruct(shape, jnp.bfloat16) for shape in PART_SHAPES],
        in_specs=[SMEM, SMEM, SMEM, HBM, HBM, HBM, VMEM, VMEM, VMEM, HBM],
        out_specs=[VMEM] + [HBM] * 10,
        scratch_shapes=stay_scratch(pool, THIRD)
        + [pltpu.VMEM(shape, jnp.bfloat16) for shape in PART_SHAPES]
        + [
            pltpu.VMEM(weight.shape, weight.dtype),
            pltpu.VMEM((2 * ROWS, weight.shape[0]), jnp.bfloat16),
            pltpu.SemaphoreType.DMA((WEIGHT_PARTS,)),
            pltpu.SemaphoreType.DMA((WEIGHT_PARTS, 4)),
        ],
        compiler_params=ROOMY,
        cost_estimate=pl.CostEstimate(flops=10**9, bytes_accessed=2**20, transcendentals=0),
        name="attend_third_project",
    )(slots, table, lengths, query, fresh, pool, first, second, returned, weight)
    return out[0], list(out[1:6]), list(out[6:])


def same_kernel(*refs):
    pass


def second_turn(up, down):
    return pl.pallas_call(
        same_kernel,
        out_shape=[jax.ShapeDtypeStruct(x.shape, x.dtype) for x in (up, down)],
        in_specs=[HBM, HBM],
        out_specs=[HBM, HBM],
        input_output_aliases={0: 0, 1: 1},
        compiler_params=PARAMS,
        cost_estimate=pl.CostEstimate(flops=3 * 10**10, bytes_accessed=2**20, transcendentals=0),
        name="second_turn",
    )(up, down)


def request_kernel(
    offset_ref, order_ref, table_ref, length_ref, query_ref, fresh_ref, out_ref, slot_ref, used
):
    own = lax.axis_index("replica")
    out_ref[...] = jnp.zeros_like(out_ref)
    for s in range(REPLICAS):
        used[s] = 0
    lane = lax.broadcasted_iota(jnp.int32, (1, HEAD), 1)
    for j in range(MIGRANTS):
        row = STAYING + j
        source = lax.rem(own + 1 + offset_ref[0, j], REPLICAS)
        rank = used[source]
        used[source] = rank + 1
        slot = source * CAP + rank
        slot_ref[j] = slot
        meta = jnp.zeros((1, HEAD), jnp.int32)
        for p in range(PAGES_ROW):
            meta = jnp.where(lane == p, table_ref[p, row], meta)
        for c in range(COPIED):
            wanted = table_ref[order_ref[j, 0, c], row]
            meta = jnp.where(lane == PAGES_ROW + c, wanted, meta)
        length = length_ref[0, row]
        meta = jnp.where(lane == 20, length // 32, meta)
        meta = jnp.where(lane == 21, lax.rem(length, 32), meta)
        out_ref[slot, 0:16] = query_ref[row - (ROWS - 16)].reshape(16, HEAD)
        out_ref[slot, 16:32] = jnp.concatenate(
            [
                fresh_ref[row - (ROWS - 16)].astype(jnp.float32).reshape(4, HEAD),
                meta.astype(jnp.float32),
                jnp.zeros((11, HEAD), jnp.float32),
            ],
            axis=0,
        ).astype(jnp.bfloat16)


def request(offsets, order, table, lengths, query, fresh):
    return pl.pallas_call(
        request_kernel,
        out_shape=(
            jax.ShapeDtypeStruct((SLOTS, 32, HEAD), jnp.bfloat16),
            jax.ShapeDtypeStruct((MIGRANTS,), jnp.int32),
        ),
        grid=(1,),
        in_specs=[SMEM] * 4
        + [pl.BlockSpec((16, 8, 2, HEAD), lambda i: (7, 0, 0, 0)), pl.BlockSpec((16, 2, 2, HEAD), lambda i: (7, 0, 0, 0))],
        out_specs=(VMEM, SMEM),
        scratch_shapes=[pltpu.SMEM((REPLICAS,), jnp.int32)],
        compiler_params=PARAMS,
        name="pack_requests",
    )(offsets, order, table, lengths, query, fresh)


def serve_kernel(
    got_ref, after_ref, pool_hbm, ret_ref, send_ref, unused_ref, pool_ref, scores_ref, pool_sem, meta_vmem, meta_ref, order_ref,
    meta_sem, page_sem
):
    fetch = fetch_pool(pool_hbm, pool_ref, pool_sem)
    for slot in range(SLOTS):
        meta_vmem[slot : slot + 1] = got_ref[slot, 16:32].astype(jnp.float32)[META_ROW : META_ROW + 1].astype(jnp.int32)
    meta_copy = pltpu.make_async_copy(meta_vmem, meta_ref, meta_sem)
    meta_copy.start()
    ret_ref[...] = jnp.zeros_like(ret_ref)
    meta_copy.wait()
    length_of = lambda slot: meta_ref[slot, 20] * 32 + meta_ref[slot, 21]
    unused = sort_rows(length_of, SLOTS, order_ref)
    unused_ref[0] = unused
    for copy in fetch:
        copy.wait()

    def copies(slot, carry):
        for c in range(COPIED):
            page = meta_ref[slot, PAGES_ROW + c]
            pltpu.make_async_copy(pool_ref.at[:, page], send_ref.at[slot, c], page_sem).start()
        return carry

    lax.fori_loop(0, SLOTS, copies, 0)

    def attend(tokens, slots):
        outputs = attend_group(
            tokens,
            [got_ref[slot, 0:16] for slot in slots],
            [got_ref[slot, 16:32].astype(jnp.float32)[0:8] for slot in slots],
            [[meta_ref[slot, p] for p in range(PAGES_ROW)] for slot in slots],
            [length_of(slot) for slot in slots],
            pool_ref,
            scores_ref,
        )
        for slot, output in zip(slots, outputs):
            ret_ref[slot] = output

    each_group((unused // GROUP, SLOTS // GROUP), order_ref, length_of, attend)
    pltpu.make_async_copy(send_ref, send_ref, page_sem).wait()


def serve(got, after, pool):
    return pl.pallas_call(
        serve_kernel,
        out_shape=(
            jax.ShapeDtypeStruct((SLOTS, 16, HEAD), jnp.bfloat16),
            jax.ShapeDtypeStruct((SLOTS, COPIED, 2, PAGE, HEAD), jnp.bfloat16),
            jax.ShapeDtypeStruct((1,), jnp.int32),
        ),
        in_specs=[VMEM, VMEM, HBM],
        out_specs=(VMEM, HBM, SMEM),
        scratch_shapes=attention_scratch(pool)
        + [
            pltpu.VMEM((SLOTS, HEAD), jnp.int32),
            pltpu.SMEM((SLOTS, HEAD), jnp.int32),
            pltpu.SMEM((SLOTS,), jnp.int32),
            pltpu.SemaphoreType.DMA,
            pltpu.SemaphoreType.DMA,
        ],
        compiler_params=ROOMY,
        cost_estimate=pl.CostEstimate(flops=6 * 10**9, bytes_accessed=8 * 2**20, transcendentals=0),
        name="serve_requests",
    )(got, after, pool)


def pick_kernel(slot_ref, got_ref, out_ref, done_ref, held, in_sem, out_sem):
    done_ref[0] = 0.0
    loads = [
        pltpu.make_async_copy(got_ref.at[slot_ref[j]], held.at[j], in_sem.at[j]) for j in range(MIGRANTS)
    ]
    stores = [pltpu.make_async_copy(held.at[j], out_ref.at[j], out_sem.at[j]) for j in range(MIGRANTS)]
    for load in loads:
        load.start()
    for load, store in zip(loads, stores):
        load.wait()
        store.start()
    for store in stores:
        store.wait()


def pick(slots, got):
    shape = (MIGRANTS, COPIED, 2, PAGE, HEAD)
    return pl.pallas_call(
        pick_kernel,
        out_shape=(jax.ShapeDtypeStruct(shape, jnp.bfloat16), jax.ShapeDtypeStruct((1,), jnp.float32)),
        in_specs=[SMEM, HBM],
        out_specs=(HBM, SMEM),
        scratch_shapes=[
            pltpu.VMEM(shape, jnp.bfloat16),
            pltpu.SemaphoreType.DMA((MIGRANTS,)),
            pltpu.SemaphoreType.DMA((MIGRANTS,)),
        ],
        compiler_params=PARAMS,
        name="pick_pages",
    )(slots, got)


def shift_z(value, by):
    pairs = [(z * 2 + x, (z + by) % 4 * 2 + x) for z in range(4) for x in range(2)]
    return lax.ppermute(value, "tensor", pairs)


def swap_x(value):
    return lax.ppermute(value, "tensor", [(t, t ^ 1) for t in range(8)])


def f32_sum(*terms):
    return functools.reduce(jnp.add, [term.astype(jnp.float32) for term in terms])


def reduce_z(own, up, down, up_later, down_later):
    from_below, from_above = shift_z(up, 1), shift_z(down, -1)
    up_later = f32_sum(up_later, from_below[:64]).astype(jnp.bfloat16)
    down_later = f32_sum(down_later, from_above[:64]).astype(jnp.bfloat16)
    first = f32_sum(own[:, :WIDTH], from_above[64:], shift_z(up_later, 1))
    second = f32_sum(own[:, WIDTH:], from_below[64:], shift_z(down_later, -1))
    return jnp.concatenate([first, second], axis=1)


def body(
    queries,
    step_key_value,
    replica_page_store,
    page_table,
    lengths,
    mig_offset,
    copy_order,
    out_weight,
):
    xi = lax.axis_index("tensor") % 2
    pool = replica_page_store[0]
    query = queries[0].reshape(ROWS, 2, 8, HEAD).transpose(0, 2, 1, 3)
    fresh = step_key_value[0]
    table = page_table[0].T
    payload, slots = request(
        mig_offset[:, :, 0], copy_order.transpose(1, 0, 2), table, lengths, query, fresh
    )
    got = lax.all_to_all(
        payload.reshape(REPLICAS, CAP, 32, HEAD), "replica", split_axis=0, concat_axis=0, tiled=True
    ).reshape(SLOTS, 32, HEAD)
    first, turn = stay(table, lengths, query, fresh, pool, FIRST)
    answered, sending, unused = serve(got, turn, pool)
    second = attend_second(unused, table, lengths, query, fresh, pool)
    returned = lax.all_to_all(
        answered.reshape(REPLICAS, CAP, 16, HEAD), "replica", split_axis=0, concat_axis=0, tiled=True
    ).reshape(SLOTS, 16, HEAD)
    incoming = lax.all_to_all(
        sending.reshape(REPLICAS, CAP, COPIED, 2, PAGE, HEAD),
        "replica",
        split_axis=0,
        concat_axis=0,
        tiled=True,
    ).reshape(SLOTS, COPIED, 2, PAGE, HEAD)
    merged, zero_parts, one_parts = project(
        slots, table, lengths, query, fresh, pool, first, second, returned, out_weight
    )
    one_parts[1:3] = second_turn(*one_parts[1:3])
    arrived, nothing = pick(slots, incoming)
    finished = []
    for parts in (zero_parts, one_parts):
        total = reduce_z(*parts).reshape(2, 32, 2 * WIDTH)
        mine = lax.dynamic_index_in_dim(total, xi, 0, keepdims=False)
        other = lax.dynamic_index_in_dim(total, 1 - xi, 0, keepdims=False)
        finished.append(mine + swap_x(other.astype(jnp.bfloat16)).astype(jnp.float32))
    finished[1] += nothing[0]
    projected = jnp.concatenate([half.astype(jnp.bfloat16) for half in finished], axis=1).reshape(16, 2, -1)
    attention = merged.transpose(0, 2, 1, 3).reshape(ROWS, 2, 8 * HEAD)
    return (attention[None], projected[None], arrived[None])


def solution(mesh):
    placed = (
        P("replica", None, None, "tensor"),
        P("replica", None, None, None, "tensor"),
        P("replica", None, None, None, "tensor"),
        P("replica", None, None),
        P("replica", None),
        P("replica", None, None),
        P("replica", None, None),
        P("tensor", None),
    )
    return jax.shard_map(
        body,
        mesh=mesh,
        in_specs=placed,
        out_specs=(
            P("replica", None, None, "tensor"),
            P("replica", "tensor", None, None),
            P("replica", None, None, None, None, "tensor"),
        ),
        check_vma=False,
    )
```
